32 devices in a mesh: groups: 2 (over x), strip: 16 (over z, y, core).
Axes of the slice: x: 2, y: 2, z: 4, core: 2. Of those that a mesh axis runs over, the one named last changes fastest.
Arguments:
- incoming_wave: float32 [8, 2, 256, 1024], P('groups', None, 'strip'), parts along dimension 0, may hold values from -64 to 64
- speed_class_map: int32 [4, 256, 1024], P('groups', 'strip'), parts along dimension 0, may hold values from 0 to 15
- spectral_entry_index: int32 [8, 4], P('groups'), parts along dimension 0, may hold values from 0 to 15
- filter_weights: float32 [16, 16, 2, 13], replicated, may hold values from -1.6 to 1.6
- scaled_pulsations: float32 [16], replicated, may hold values from 1 to 6
- inverse_speed_classes: float32 [16], replicated, may hold values from 0.3 to 1.5
Outputs:
- image: float32 [4, 256, 1024], P('groups', 'strip'), parts along dimension 0
- handed: float32 [8, 2, 256, 1024], P('groups', None, 'strip'), parts along dimension 0
The draws below stay inside these ranges and needn't reach their ends.
There are 2 independent parts, one for each index of `groups`. The reference program is written for one: setup_inputs(seed, part) draws one part's arguments, and reference() takes and returns one part's arrays. A program takes and returns all parts, laid end to end along the dimension named above; an argument that names none is the same for every part. Nothing has to cross between parts.
All inputs are finite; a program needn't handle non-finite values.
Results may differ from the reference program's by a relative error of at most 0.0003.
Values sent between devices are 32-bit elements; how exact they have to be, the bound alone decides.
No kernel may reach another device: no remote copies, remote signals or barrier semaphores. Data moves between devices by JAX's collectives and lax.ppermute only.
A program may use at most 128 MiB of HBM per device.

```python
import math
import jax
import jax.numpy as jnp
from jax import lax

NY = 1024
SECTIONS = 4
LEVELS = 2
ORDER = 12
NFREQ = 4
NBIN = 16
NW = 16
SIDEWAYS_COUNT = 64


def draw_incoming_wave(key, part):
    noise_key = jax.random.fold_in(jax.random.fold_in(key, 11), 0)
    total_rows = SECTIONS * SIDEWAYS_COUNT
    shifted_rows = (jnp.arange(total_rows, dtype=jnp.int32) - SIDEWAYS_COUNT // 2) % total_rows
    position = (shifted_rows % SIDEWAYS_COUNT).astype(jnp.float32) / max(SIDEWAYS_COUNT - 1, 1)
    profile = jnp.exp(jnp.log(3.0) * position)[None, None, :, None]
    base = jnp.clip(jax.random.normal(noise_key, (NFREQ, 2, total_rows, NY), jnp.float32), -6.0, 6.0)
    return base * profile


def touch_ends(values, rng, smallest, top_value):
    longest = values.shape.index(max(values.shape))
    spots = []
    for shift in (0, 1):
        where = [jax.random.randint(jax.random.fold_in(rng, axis), (), 0, length) for axis, length in enumerate(values.shape)]
        where[longest] = (where[longest] + shift) % values.shape[longest]
        spots.append(tuple(where))
    return values.at[spots[0]].set(smallest).at[spots[1]].set(top_value)


def scatter_about(own_key, dims, spread, bound, kind=jnp.bfloat16):
    drawn = spread * jax.random.normal(own_key, dims, jnp.float32)
    return jnp.clip(drawn, min=-bound, max=bound).astype(kind)


def setup_inputs(seed: int = 0, part: int = 0) -> dict:
    streams_of = jax.random.split(jax.random.key(seed), 7)
    part_splits = jax.random.split(jax.random.fold_in(streams_of[6], part), 7)
    return {
        "incoming_wave": draw_incoming_wave(jax.random.fold_in(jax.random.fold_in(streams_of[6], part), 71), part),
        "speed_class_map": touch_ends(jax.random.randint(part_splits[1], (LEVELS, SECTIONS * SIDEWAYS_COUNT, NY), 0, NBIN), jax.random.fold_in(part_splits[1], 1), 0, NBIN - 1).astype(jnp.int32),
        "spectral_entry_index": touch_ends(jax.random.randint(part_splits[2], (SECTIONS, NFREQ), 0, NW), jax.random.fold_in(part_splits[2], 1), 0, NW - 1).astype(jnp.int32),
        "filter_weights": scatter_about(streams_of[3], (NW, NBIN, 2, ORDER + 1), 0.28, 1.6, jnp.float32),
        "scaled_pulsations": jnp.clip(jnp.exp(jax.random.uniform(streams_of[4], (NW,), jnp.float32, math.log(1.0), math.log(6.0))), 1.0, 6.0),
        "inverse_speed_classes": jnp.clip(jnp.exp(jax.random.uniform(streams_of[5], (NBIN,), jnp.float32, math.log(0.3), math.log(1.5))), 0.3, 1.5),
    }


def stencil_padded(padded):
    vertical = padded[:, :, :-2, :] + padded[:, :, 2:, :]
    middle = padded[:, :, 1:-1, :]
    return -0.5 * middle[..., 1:-1] + 0.25 * (vertical[..., 1:-1] + middle[..., :-2] + middle[..., 2:]) + 0.125 * (vertical[..., :-2] + vertical[..., 2:])

def mcclellan_step(field):
    return stencil_padded(jnp.pad(field, ((0, 0), (0, 0), (1, 1), (1, 1))))

def complex_times(coeff, field):
    real_part = coeff[:, 0] * field[:, 0] - coeff[:, 1] * field[:, 1]
    imag_part = coeff[:, 0] * field[:, 1] + coeff[:, 1] * field[:, 0]
    return jnp.stack([real_part, imag_part], axis=1)

def image_downward(field, speed_strata, freq_row, filter_weights, scaled_pulsations, inverse_speed_classes):
    highest = lax.Precision.HIGHEST
    freq_select = (freq_row[:, None] == jnp.arange(NW, dtype=jnp.int32)[None, :]).astype(jnp.float32)
    freq_coeffs = jnp.einsum('fw,wbck->fbck', freq_select, filter_weights, precision=highest)
    freq_omega = jnp.dot(freq_select, scaled_pulsations, precision=highest)
    wavefield = field
    raws = []
    for level in range(LEVELS):
        cells = speed_strata[level].reshape(-1)
        bin_onehot = (cells[None, :] == jnp.arange(NBIN, dtype=jnp.int32)[:, None]).astype(jnp.float32)
        cell_slowness = jnp.dot(inverse_speed_classes, bin_onehot, precision=highest).reshape(SIDEWAYS_COUNT, NY)
        table = jnp.einsum('fbck,bn->kfcn', freq_coeffs, bin_onehot, precision=highest).reshape(ORDER + 1, NFREQ, 2, SIDEWAYS_COUNT, NY)
        previous = wavefield
        current = mcclellan_step(wavefield)
        accumulated = complex_times(table[0], previous) + complex_times(table[1], current)
        for order_index in range(2, ORDER + 1):
            following = 2.0 * mcclellan_step(current) - previous
            accumulated = accumulated + complex_times(table[order_index], following)
            previous, current = (current, following)
        phase_angle = freq_omega[:, None, None] * cell_slowness[None]
        cosine = jnp.cos(phase_angle)
        sine_part = jnp.sin(phase_angle)
        real_part = accumulated[:, 0] * cosine - accumulated[:, 1] * sine_part
        imag_part = accumulated[:, 0] * sine_part + accumulated[:, 1] * cosine
        wavefield = jnp.stack([real_part, imag_part], axis=1)
        raws.append(lax.optimization_barrier(jnp.sum(real_part, axis=0)))
    return (wavefield, raws)

def reference(incoming_wave, speed_class_map, spectral_entry_index, filter_weights, scaled_pulsations, inverse_speed_classes):
    half_shift = SIDEWAYS_COUNT // 2
    incoming_wave = jnp.roll(incoming_wave, -half_shift, axis=2)
    speed_class_map = jnp.roll(speed_class_map, -half_shift, axis=1)
    bottoms = []
    images = []
    handed_parts = []
    for vertical_slab in range(SECTIONS):
        speed_strata = speed_class_map[:, vertical_slab * SIDEWAYS_COUNT:(vertical_slab + 1) * SIDEWAYS_COUNT, :]
        above_floor_lines, above_unscaled_waves = image_downward(incoming_wave[:, :, vertical_slab * SIDEWAYS_COUNT:(vertical_slab + 1) * SIDEWAYS_COUNT, :], speed_strata, spectral_entry_index[vertical_slab], filter_weights, scaled_pulsations, inverse_speed_classes)
        bottoms.append(above_floor_lines)
        if vertical_slab == 0:
            totals = above_unscaled_waves
            handed_parts.append(above_floor_lines)
        else:
            second_bottom, second_raws = image_downward(bottoms[vertical_slab - 1], speed_strata, spectral_entry_index[vertical_slab - 1], filter_weights, scaled_pulsations, inverse_speed_classes)
            totals = [above_unscaled_waves[level] + second_raws[level] for level in range(LEVELS)]
            handed_parts.append(second_bottom)
        section_images = []
        for level in range(LEVELS):
            raw_image = totals[level]
            mean_square = jnp.sum(raw_image * raw_image) / (SIDEWAYS_COUNT * NY)
            section_images.append(raw_image / jnp.sqrt(mean_square + 1e-06))
        images.append(jnp.stack(section_images, axis=0))
    image = jnp.roll(jnp.concatenate(images, axis=1), half_shift, axis=1)
    handed = jnp.roll(jnp.concatenate(handed_parts, axis=2), half_shift, axis=2)
    return (image, handed)
```

```python
import functools

import jax
import jax.numpy as jnp
from jax import lax
from jax.experimental import pallas as pl
from jax.experimental.pallas import tpu as pltpu
from jax.sharding import PartitionSpec as P

SECTIONS = 4
LEVELS = 2
ORDER = 12
NFREQ = 4
NBIN = 16
NW = 16


def extended_2(shard, sides, width):
    for axis, dim in sides:
        devices, length = (lax.axis_size(axis), shard.shape[dim])
        up = [(i, (i + 1) % devices) for i in range(devices)]
        down = [(j, i) for i, j in up]
        last = lax.slice_in_dim(shard, length - width, length, axis=dim)
        initial = lax.slice_in_dim(shard, 0, width, axis=dim)
        before = lax.ppermute(last, axis, up)
        after = lax.ppermute(initial, axis, down)
        shard = jnp.concatenate([before, shard, after], axis=dim)
    return shard


def from_behind(shard, axis, by):
    devices = lax.axis_size(axis)
    return lax.ppermute(shard, axis, [(i, (i + by) % devices) for i in range(devices)])


def stencil_padded(padded):
    vertical = padded[:, :, :-2, :] + padded[:, :, 2:, :]
    middle = padded[:, :, 1:-1, :]
    return (
        -0.5 * middle[..., 1:-1]
        + 0.25 * (vertical[..., 1:-1] + middle[..., :-2] + middle[..., 2:])
        + 0.125 * (vertical[..., :-2] + vertical[..., 2:])
    )


def complex_times(coeff, field):
    real_part = coeff[:, 0] * field[:, 0] - coeff[:, 1] * field[:, 1]
    imag_part = coeff[:, 0] * field[:, 1] + coeff[:, 1] * field[:, 0]
    return jnp.stack([real_part, imag_part], axis=1)


def strip_shards(
    incoming_wave,
    speed_class_map,
    spectral_entry_index,
    filter_weights,
    scaled_pulsations,
    inverse_speed_classes,
):
    highest = lax.Precision.HIGHEST
    summed_along = incoming_wave.shape[2]
    summed_across = incoming_wave.shape[3]
    strip_count = lax.axis_size("strip")
    lateral_count = strip_count // SECTIONS
    position = (lax.axis_index("strip") - lateral_count // 2) % strip_count
    vertical_slab = position // lateral_count
    lateral_place = position % lateral_count
    section_rows = summed_along * lateral_count
    section_cells = section_rows * summed_across
    margin = ORDER
    extended_rows = summed_along + 2 * margin
    lateral_rows = (
        lateral_place * summed_along - margin + jnp.arange(extended_rows, dtype=jnp.int32)
    )
    inside = ((lateral_rows >= 0) & (lateral_rows < section_rows)).astype(jnp.float32)[
        None, None, :, None
    ]

    def mcclellan_step(field):
        padded = jnp.pad(field, ((0, 0), (0, 0), (1, 1), (0, 0)))
        padded = jnp.pad(padded, ((0, 0), (0, 0), (0, 0), (1, 1)))
        result = stencil_padded(padded)
        result = result * inside
        return result

    def interior(field):
        return field[:, :, margin : margin + summed_along, :]

    def image_downward(field, batch_index):
        freq_row = lax.dynamic_index_in_dim(spectral_entry_index, batch_index, 0, keepdims=False)
        freq_select = (freq_row[:, None] == jnp.arange(NW, dtype=jnp.int32)[None, :]).astype(
            jnp.float32
        )
        freq_coeffs = jnp.einsum("fw,wbck->fbck", freq_select, filter_weights, precision=highest)
        freq_omega = jnp.dot(freq_select, scaled_pulsations, precision=highest)
        wavefield = field
        raws = []
        for level in range(LEVELS):
            cells = speed_class_map[level].reshape(-1)
            bin_onehot = (cells[None, :] == jnp.arange(NBIN, dtype=jnp.int32)[:, None]).astype(
                jnp.float32
            )
            cell_slowness = jnp.dot(inverse_speed_classes, bin_onehot, precision=highest).reshape(
                summed_along, summed_across
            )
            table = jnp.einsum("fbck,bn->kfcn", freq_coeffs, bin_onehot, precision=highest).reshape(
                ORDER + 1, NFREQ, 2, summed_along, summed_across
            )
            extended = extended_2(wavefield, (("strip", 2),), ORDER) * inside
            previous = extended
            current = mcclellan_step(extended)
            accumulated = complex_times(table[0], interior(previous)) + complex_times(
                table[1], interior(current)
            )

            def recursion_step(order_index, state_tuple):
                before, present, running = state_tuple
                following = 2.0 * mcclellan_step(present) - before
                coeff = lax.dynamic_index_in_dim(table, order_index, 0, keepdims=False)
                running = running + complex_times(coeff, interior(following))
                return (present, following, running)

            previous, current, accumulated = lax.fori_loop(
                2, ORDER + 1, recursion_step, (previous, current, accumulated)
            )
            phase_angle = freq_omega[:, None, None] * cell_slowness[None]
            cosine = jnp.cos(phase_angle)
            sine_part = jnp.sin(phase_angle)
            real_part = accumulated[:, 0] * cosine - accumulated[:, 1] * sine_part
            imag_part = accumulated[:, 0] * sine_part + accumulated[:, 1] * cosine
            wavefield = jnp.stack([real_part, imag_part], axis=1)
            raws.append(jnp.sum(real_part, axis=0))
        return (wavefield, raws)

    above_floor_lines, above_unscaled_waves = image_downward(incoming_wave, vertical_slab)
    arriving = from_behind(above_floor_lines, "strip", lateral_count)
    second_bottom, second_raws = image_downward(arriving, jnp.maximum(vertical_slab - 1, 0))
    handed = jnp.where(vertical_slab == 0, above_floor_lines, second_bottom)
    first_section = (vertical_slab > 0).astype(jnp.float32)
    totals = [
        above_unscaled_waves[level] + first_section * second_raws[level] for level in range(LEVELS)
    ]
    selector = (jnp.arange(SECTIONS, dtype=jnp.int32) == vertical_slab).astype(jnp.float32)
    images = []
    for level in range(LEVELS):
        raw_image = totals[level]
        spread = lax.psum(selector * jnp.sum(raw_image * raw_image), "strip")
        mean_square = jnp.sum(spread * selector) / section_cells
        images.append(raw_image / jnp.sqrt(mean_square + 1e-06))
    return (jnp.stack(images, axis=0), handed)


LANES = 128
SUB = 8


def cell(i, j):
    return (j, pl.ds(SUB * i, SUB), slice(None))


def column(j):
    return pl.ds(LANES * j, LANES)


def rim(src, plane, tiles):
    sub = lax.broadcasted_iota(jnp.int32, (SUB, LANES), 0)
    lower, upper, rows = [], [], []
    for j in range(tiles):
        v0 = src[(plane,) + cell(0, j)]
        v7 = src[(plane,) + cell(SUB - 1, j)]
        p = v7 + jnp.where(sub == SUB - 1, 0.0, pltpu.roll(v0, SUB - 1, 0))
        lower.append(p)
        upper.append(jnp.where(sub == 0, v0, pltpu.roll(p, 1, 0)))
        rows.append(v0)
    return lower, upper, rows


def across(w):
    lane = lax.broadcasted_iota(jnp.int32, (SUB, LANES), 1)
    tiles = len(w)
    q = [w[j] + w[j + 1] for j in range(tiles - 1)]
    q.append(w[-1] + jnp.where(lane == LANES - 1, 0.0, pltpu.roll(w[0], LANES - 1, 1)))
    before = jnp.where(lane == 0, w[0], pltpu.roll(q[-1], 1, 1))
    return [q[j] + (q[j - 1] if j else before) for j in range(tiles)]


def weighted(table, cells, k, i, j):
    index = cells[cell(i, j)]
    return (
        jnp.take_along_axis(table[k, 0], index, axis=1),
        jnp.take_along_axis(table[k, 1], index, axis=1),
    )


def advance(src, other, total, cells, table, k, tiles, first=False, mac=False):
    edges = [rim(src, plane, tiles) for plane in range(2)]
    above = [e[1] for e in edges]
    present = [e[2] for e in edges]
    for i in range(SUB):
        new, old = [], []
        for plane in range(2):
            if i < SUB - 1:
                below = [src[(plane,) + cell(i + 1, j)] for j in range(tiles)]
                pairs = [present[plane][j] + below[j] for j in range(tiles)]
            else:
                below = None
                pairs = edges[plane][0]
            h = across([pairs[j] + above[plane][j] for j in range(tiles)])
            above[plane] = pairs
            out = []
            for j in range(tiles):
                at = (plane,) + cell(i, j)
                v = present[plane][j]
                u = v - 0.125 * h[j] if first else (v + v) - (0.25 * h[j] + other[at])
                other[at] = u
                out.append(u)
            old.append(present[plane])
            present[plane] = below
            new.append(out)
        if mac:
            for j in range(tiles):
                c0r, c0i = weighted(table, cells, k, i, j)
                c1r, c1i = weighted(table, cells, k + 1, i, j)
                ur, ui = new[0][j], new[1][j]
                vr, vi = old[0][j], old[1][j]
                a = (c1r * ur - c1i * ui) + (c0r * vr - c0i * vi)
                b = (c1r * ui + c1i * ur) + (c0r * vi + c0i * vr)
                re, im = (0,) + cell(i, j), (1,) + cell(i, j)
                if first:
                    total[re], total[im] = a, b
                else:
                    total[re] = total[re] + a
                    total[im] = total[im] + b


def one_level(src, even, odd, total, cells, table, tiles):
    advance(src, odd, total, cells, table, 0, tiles, first=True, mac=True)
    for plane in range(2):
        for i in range(SUB):
            for j in range(tiles):
                even[(plane,) + cell(i, j)] = src[(plane,) + cell(i, j)]

    def pair(t, carry):
        k = 2 * t + 1
        advance(odd, even, total, cells, table, k, tiles)
        advance(even, odd, total, cells, table, k + 1, tiles, mac=True)
        return carry

    lax.fori_loop(0, ORDER // 2 - 1, pair, 0)
    advance(odd, even, total, cells, table, ORDER - 1, tiles)
    for i in range(SUB):
        for j in range(tiles):
            cr, ci = weighted(table, cells, ORDER, i, j)
            re, im = (0,) + cell(i, j), (1,) + cell(i, j)
            ur, ui = even[re], even[im]
            total[re] = total[re] + (cr * ur - ci * ui)
            total[im] = total[im] + (cr * ui + ci * ur)


def fold(block, turned, tiles):
    for j in range(tiles):
        turned[column(j), :] = block[:, column(j)].T
    return [turned[pl.ds(j, LANES, stride=tiles), :].T for j in range(tiles)]


def unfold(block, turned, tiles):
    for j in range(tiles):
        turned[pl.ds(j, LANES, stride=tiles), :] = block[:, column(j)].T
    return [turned[column(j), :].T for j in range(tiles)]


def folded_cells(lane_ref, own, across_chip, core_pair, natural, block, turned, cells, tiles):
    here = lane_ref[0]
    rows = own.shape[2]
    strips = (here ^ 2, here, here ^ 3, here ^ 1)
    pieces = (own, across_chip, core_pair.at[0], core_pair.at[1])
    for piece, strip in zip(pieces, strips):
        at = pl.ds(pl.multiple_of(strip * rows, rows), rows)
        for level in range(LEVELS):
            for which in range(2):
                for j in range(tiles):
                    natural[which * LEVELS + level, j, at, :] = piece[which, level, :, column(j)]
    for which in range(2):
        for level in range(LEVELS):
            for i in range(SUB):
                for j in range(tiles):
                    block[pl.ds(64 * level + SUB * i, SUB), column(j)] = natural[
                        which * LEVELS + level, j, pl.ds(i, SUB, stride=SUB), :
                    ].astype(jnp.float32)
        for j, tile in enumerate(fold(block, turned, tiles)):
            for level in range(LEVELS):
                cells[which * LEVELS + level, j] = tile[64 * level : 64 * level + 64].astype(
                    jnp.int32
                )


def cells_kernel(lane_ref, own, across_chip, core_pair, cells, natural, block, turned):
    folded_cells(
        lane_ref, own, across_chip, core_pair, natural, block, turned, cells, cells.shape[1]
    )


def rows_out(level_total, bottom, natural, outs, here, rows):
    for j in range(bottom.shape[1]):
        for g in range(SUB):
            at = pl.ds(SUB * g, SUB)
            natural[0, j, at, :] = level_total[0, j, pl.ds(g, SUB, stride=SUB), :]
            natural[1, j, at, :] = bottom[0, j, pl.ds(g, SUB, stride=SUB), :]
            natural[2, j, at, :] = bottom[1, j, pl.ds(g, SUB, stride=SUB), :]
    for r, out in enumerate(outs):
        at = pl.ds(pl.multiple_of((here ^ r ^ 2) * rows, rows), rows)
        for plane in range(3):
            for j in range(bottom.shape[1]):
                out[plane, :, column(j)] = natural[plane, j, at, :]


def upper_kernel(
    lane_ref, w0, w1, w2, w3, cells, table, bottom, o0, o1, o2, o3, first, even, odd, block, turned, natural
):
    here = lane_ref[0]
    rows = w0.shape[1]
    tiles = w0.shape[2] // LANES
    for r, piece in enumerate((w0, w1, w2, w3)):
        at = pl.ds(pl.multiple_of((here ^ r ^ 2) * rows, rows), rows)
        for plane in range(2):
            for j in range(tiles):
                natural[plane, j, at, :] = piece[plane, :, column(j)]
    for plane in range(2):
        for i in range(SUB):
            for j in range(tiles):
                block[pl.ds(64 * plane + SUB * i, SUB), column(j)] = natural[
                    plane, j, pl.ds(i, SUB, stride=SUB), :
                ]
    for j, tile in enumerate(fold(block, turned, tiles)):
        for plane in range(2):
            bottom[plane, j] = tile[64 * plane : 64 * plane + 64]
    one_level(bottom, even, odd, first, cells.at[0], table, tiles)
    one_level(first, even, odd, bottom, cells.at[1], table, tiles)
    rows_out(first, bottom, natural, (o0, o1, o2, o3), here, rows)


def lower_kernel(lane_ref, wave, cells, table, o0, o1, o2, o3, first, second, even, odd, natural):
    here = lane_ref[0]
    tiles = wave.shape[1]
    one_level(wave, even, odd, first, cells.at[LEVELS], table, tiles)
    one_level(first, even, odd, second, cells.at[LEVELS + 1], table, tiles)
    rows_out(first, second, natural, (o0, o1, o2, o3), here, o0.shape[1])


def final_kernel(
    lane_ref, m0, m1, m2, m3, n0, n1, n2, n3, handed, raw, squares, block, turned, picture
):
    here, top = lane_ref[0], lane_ref[1] == 0
    rows = m0.shape[1]
    tiles = m0.shape[2] // LANES
    sums = []
    for level in range(LEVELS):
        early = (n0[level] + n1[level]) + (n2[level] + n3[level])
        late = (m0[level] + m1[level]) + (m2[level] + m3[level])
        total = jnp.where(top, early, early + late)
        picture[pl.ds(rows * level, rows), :] = total
        sums.append(jnp.sum(total * total))
    lane = lax.broadcasted_iota(jnp.int32, (SUB, LANES), 1)
    squares[...] = jnp.where(lane == 0, sums[0], jnp.where(lane == 1, sums[1], 0.0))
    for r, (m, n) in enumerate(zip((m0, m1, m2, m3), (n0, n1, n2, n3))):
        at = (here ^ r) * (2 * rows)
        for plane in range(2):
            block[pl.ds(pl.multiple_of(at + plane * rows, rows), rows), :] = jnp.where(
                top, n[1 + plane], m[1 + plane]
            )
    for j, tile in enumerate(unfold(block, turned, tiles)):
        for f in range(NFREQ):
            for plane in range(2):
                start = (2 * f + plane) * rows
                handed[f, plane, :, column(j)] = tile[start : start + rows]
    for j, tile in enumerate(unfold(picture, turned, tiles)):
        for level in range(LEVELS):
            raw[level, :, column(j)] = tile[rows * level : rows * level + rows]


def call(kernel, outs, scratch, *operands):
    vmem = pl.BlockSpec(memory_space=pltpu.VMEM)
    smem = pl.BlockSpec(memory_space=pltpu.SMEM)
    return pl.pallas_call(
        kernel,
        out_shape=outs,
        in_specs=[smem] + [vmem] * (len(operands) - 1),
        out_specs=[vmem] * len(outs),
        scratch_shapes=scratch,
        compiler_params=pltpu.CompilerParams(vmem_limit_bytes=40 << 20),
    )(*operands)


def frequency_shards(
    incoming_wave,
    speed_class_map,
    spectral_entry_index,
    filter_weights,
    scaled_pulsations,
    inverse_speed_classes,
):
    devices = lax.axis_size("strip")
    rows, columns = incoming_wave.shape[2], incoming_wave.shape[3]
    me = lax.axis_index("strip")
    plane, here = me // NFREQ, me % NFREQ
    planes = devices // NFREQ

    def place(p, lane):
        return (p % planes) * NFREQ + lane

    everyone = [(p, lane) for p in range(planes) for lane in range(NFREQ)]

    def send(value, pairs):
        return lax.ppermute(value, "strip", pairs)

    far = send(
        speed_class_map,
        [(place(p, lane), place(p + (1 if lane >= 2 else -1), lane)) for p, lane in everyone],
    )
    starts = [
        send(
            lax.dynamic_index_in_dim(incoming_wave, here ^ r, 0, keepdims=False),
            [(place(p, lane), place(p + lane // 2, lane ^ r)) for p, lane in everyone],
        )
        for r in range(NFREQ)
    ]
    upper_half = here >= 2
    own = jnp.stack(
        [
            jnp.where(upper_half, far, speed_class_map),
            jnp.where(upper_half, speed_class_map, far),
        ]
    )
    across_chip = send(own, [(place(p, lane), place(p, lane ^ 2)) for p, lane in everyone])
    core_pair = send(
        jnp.stack([own, across_chip]), [(place(p, lane), place(p, lane ^ 1)) for p, lane in everyone]
    )

    section = (plane - 1) % planes
    entry = spectral_entry_index[section, here]
    weights = lax.dynamic_index_in_dim(filter_weights, entry, 0, keepdims=False)
    pulsation = scaled_pulsations[entry]
    angle = pulsation * inverse_speed_classes
    cosine, sine = jnp.cos(angle)[:, None], jnp.sin(angle)[:, None]
    sign = 1.0 - 2.0 * (jnp.arange(ORDER + 1) % 2).astype(jnp.float32)
    real = (weights[:, 0] * cosine - weights[:, 1] * sine) * sign
    imag = (weights[:, 0] * sine + weights[:, 1] * cosine) * sign
    table = jnp.stack([real, imag], axis=0).transpose(2, 0, 1)
    table = jnp.pad(table, ((0, 0), (0, 0), (0, LANES - NBIN)))
    table = jnp.broadcast_to(table[:, :, None, :], (ORDER + 1, 2, SUB, LANES))

    owned = (plane - jnp.where(upper_half, 0, 1)) % planes
    lanes = jnp.stack([here, owned]).astype(jnp.int32)
    field = (2, columns // LANES, SUB * SUB, LANES)
    natural = pltpu.VMEM((3,) + field[1:], jnp.float32)
    half = pltpu.VMEM(field, jnp.float32)
    turned = pltpu.VMEM((columns, LANES), jnp.float32)
    block = pltpu.VMEM((LANES, columns), jnp.float32)
    shape = jax.ShapeDtypeStruct
    message = shape((3, rows, columns), jnp.float32)

    (cells,) = call(
        cells_kernel,
        [shape((2 * LEVELS,) + field[1:], jnp.int32)],
        [pltpu.VMEM((2 * LEVELS,) + field[1:], jnp.int32), block, turned],
        lanes,
        own,
        across_chip,
        core_pair,
    )
    bottom, *early = call(
        upper_kernel,
        [shape(field, jnp.float32)] + [message] * NFREQ,
        [half, half, half, block, turned, natural],
        lanes,
        *starts,
        cells,
        table,
    )
    early = [
        send(v, [(place(p, lane), place(p - (lane ^ r) // 2, lane ^ r)) for p, lane in everyone])
        for r, v in enumerate(early)
    ]
    late = call(
        lower_kernel,
        [message] * NFREQ,
        [half, half, half, half, natural],
        lanes,
        bottom,
        cells,
        table,
    )
    late = [
        send(v, [(place(p, lane), place(p + 1 - (lane ^ r) // 2, lane ^ r)) for p, lane in everyone])
        for r, v in enumerate(late)
    ]
    handed, raw, squares = call(
        final_kernel,
        [
            shape(incoming_wave.shape, jnp.float32),
            shape(speed_class_map.shape, jnp.float32),
            shape((SUB, LANES), jnp.float32),
        ],
        [block, turned, block],
        lanes,
        *late,
        *early,
    )

    def owner(s, strip):
        return place(s + strip // 2, strip ^ 2)

    mean_square = squares
    for r in range(1, NFREQ):
        mean_square = mean_square + send(
            squares,
            [(owner(s, strip), owner(s, strip ^ r)) for s in range(planes) for strip in range(NFREQ)],
        )
    mean_square = mean_square[0, :LEVELS] / (rows * NFREQ * columns)
    image = raw / jnp.sqrt(mean_square + 1e-06)[:, None, None]
    return (image, handed)


def shards(*operands):
    lateral_count = lax.axis_size("strip") // SECTIONS
    rows, columns = operands[0].shape[2:]
    if lateral_count == NFREQ and rows * lateral_count == SUB * SUB and columns == SUB * LANES:
        return frequency_shards(*operands)
    return strip_shards(*operands)


def solution(mesh):
    return jax.shard_map(
        shards,
        mesh=mesh,
        in_specs=(
            P("groups", None, "strip", None),
            P("groups", "strip", None),
            P("groups", None),
            P(),
            P(),
            P(),
        ),
        out_specs=(P("groups", "strip", None), P("groups", None, "strip", None)),
        check_vma=False,
    )
```

```python
import functools

import jax
import jax.numpy as jnp
from jax import lax
from jax.experimental import pallas as pl
from jax.experimental.pallas import tpu as pltpu
from jax.sharding import PartitionSpec as P

SECTIONS = 4
LEVELS = 2
ORDER = 12
NFREQ = 4
NBIN = 16
NW = 16


def extended_2(shard, sides, width):
    for axis, dim in sides:
        devices, length = (lax.axis_size(axis), shard.shape[dim])
        up = [(i, (i + 1) % devices) for i in range(devices)]
        down = [(j, i) for i, j in up]
        last = lax.slice_in_dim(shard, length - width, length, axis=dim)
        initial = lax.slice_in_dim(shard, 0, width, axis=dim)
        before = lax.ppermute(last, axis, up)
        after = lax.ppermute(initial, axis, down)
        shard = jnp.concatenate([before, shard, after], axis=dim)
    return shard


def from_behind(shard, axis, by):
    devices = lax.axis_size(axis)
    return lax.ppermute(shard, axis, [(i, (i + by) % devices) for i in range(devices)])


def stencil_padded(padded):
    vertical = padded[:, :, :-2, :] + padded[:, :, 2:, :]
    middle = padded[:, :, 1:-1, :]
    return (
        -0.5 * middle[..., 1:-1]
        + 0.25 * (vertical[..., 1:-1] + middle[..., :-2] + middle[..., 2:])
        + 0.125 * (vertical[..., :-2] + vertical[..., 2:])
    )


def complex_times(coeff, field):
    real_part = coeff[:, 0] * field[:, 0] - coeff[:, 1] * field[:, 1]
    imag_part = coeff[:, 0] * field[:, 1] + coeff[:, 1] * field[:, 0]
    return jnp.stack([real_part, imag_part], axis=1)


def strip_shards(
    incoming_wave,
    speed_class_map,
    spectral_entry_index,
    filter_weights,
    scaled_pulsations,
    inverse_speed_classes,
):
    highest = lax.Precision.HIGHEST
    summed_along = incoming_wave.shape[2]
    summed_across = incoming_wave.shape[3]
    strip_count = lax.axis_size("strip")
    lateral_count = strip_count // SECTIONS
    position = (lax.axis_index("strip") - lateral_count // 2) % strip_count
    vertical_slab = position // lateral_count
    lateral_place = position % lateral_count
    section_rows = summed_along * lateral_count
    section_cells = section_rows * summed_across
    margin = ORDER
    extended_rows = summed_along + 2 * margin
    lateral_rows = (
        lateral_place * summed_along - margin + jnp.arange(extended_rows, dtype=jnp.int32)
    )
    inside = ((lateral_rows >= 0) & (lateral_rows < section_rows)).astype(jnp.float32)[
        None, None, :, None
    ]

    def mcclellan_step(field):
        padded = jnp.pad(field, ((0, 0), (0, 0), (1, 1), (0, 0)))
        padded = jnp.pad(padded, ((0, 0), (0, 0), (0, 0), (1, 1)))
        result = stencil_padded(padded)
        result = result * inside
        return result

    def interior(field):
        return field[:, :, margin : margin + summed_along, :]

    def image_downward(field, batch_index):
        freq_row = lax.dynamic_index_in_dim(spectral_entry_index, batch_index, 0, keepdims=False)
        freq_select = (freq_row[:, None] == jnp.arange(NW, dtype=jnp.int32)[None, :]).astype(
            jnp.float32
        )
        freq_coeffs = jnp.einsum("fw,wbck->fbck", freq_select, filter_weights, precision=highest)
        freq_omega = jnp.dot(freq_select, scaled_pulsations, precision=highest)
        wavefield = field
        raws = []
        for level in range(LEVELS):
            cells = speed_class_map[level].reshape(-1)
            bin_onehot = (cells[None, :] == jnp.arange(NBIN, dtype=jnp.int32)[:, None]).astype(
                jnp.float32
            )
            cell_slowness = jnp.dot(inverse_speed_classes, bin_onehot, precision=highest).reshape(
                summed_along, summed_across
            )
            table = jnp.einsum("fbck,bn->kfcn", freq_coeffs, bin_onehot, precision=highest).reshape(
                ORDER + 1, NFREQ, 2, summed_along, summed_across
            )
            extended = extended_2(wavefield, (("strip", 2),), ORDER) * inside
            previous = extended
            current = mcclellan_step(extended)
            accumulated = complex_times(table[0], interior(previous)) + complex_times(
                table[1], interior(current)
            )

            def recursion_step(order_index, state_tuple):
                before, present, running = state_tuple
                following = 2.0 * mcclellan_step(present) - before
                coeff = lax.dynamic_index_in_dim(table, order_index, 0, keepdims=False)
                running = running + complex_times(coeff, interior(following))
                return (present, following, running)

            previous, current, accumulated = lax.fori_loop(
                2, ORDER + 1, recursion_step, (previous, current, accumulated)
            )
            phase_angle = freq_omega[:, None, None] * cell_slowness[None]
            cosine = jnp.cos(phase_angle)
            sine_part = jnp.sin(phase_angle)
            real_part = accumulated[:, 0] * cosine - accumulated[:, 1] * sine_part
            imag_part = accumulated[:, 0] * sine_part + accumulated[:, 1] * cosine
            wavefield = jnp.stack([real_part, imag_part], axis=1)
            raws.append(jnp.sum(real_part, axis=0))
        return (wavefield, raws)

    above_floor_lines, above_unscaled_waves = image_downward(incoming_wave, vertical_slab)
    arriving = from_behind(above_floor_lines, "strip", lateral_count)
    second_bottom, second_raws = image_downward(arriving, jnp.maximum(vertical_slab - 1, 0))
    handed = jnp.where(vertical_slab == 0, above_floor_lines, second_bottom)
    first_section = (vertical_slab > 0).astype(jnp.float32)
    totals = [
        above_unscaled_waves[level] + first_section * second_raws[level] for level in range(LEVELS)
    ]
    selector = (jnp.arange(SECTIONS, dtype=jnp.int32) == vertical_slab).astype(jnp.float32)
    images = []
    for level in range(LEVELS):
        raw_image = totals[level]
        spread = lax.psum(selector * jnp.sum(raw_image * raw_image), "strip")
        mean_square = jnp.sum(spread * selector) / section_cells
        images.append(raw_image / jnp.sqrt(mean_square + 1e-06))
    return (jnp.stack(images, axis=0), handed)


LANES = 128
SUB = 8


def cell(i, j):
    return (j, pl.ds(SUB * i, SUB), slice(None))


def column(j):
    return pl.ds(LANES * j, LANES)


def rim(src, plane, tiles):
    sub = lax.broadcasted_iota(jnp.int32, (SUB, LANES), 0)
    lower, upper, rows = [], [], []
    for j in range(tiles):
        v0 = src[(plane,) + cell(0, j)]
        v7 = src[(plane,) + cell(SUB - 1, j)]
        p = v7 + jnp.where(sub == SUB - 1, 0.0, pltpu.roll(v0, SUB - 1, 0))
        lower.append(p)
        upper.append(jnp.where(sub == 0, v0, pltpu.roll(p, 1, 0)))
        rows.append(v0)
    return lower, upper, rows


def across(w):
    lane = lax.broadcasted_iota(jnp.int32, (SUB, LANES), 1)
    tiles = len(w)
    q = [w[j] + w[j + 1] for j in range(tiles - 1)]
    q.append(w[-1] + jnp.where(lane == LANES - 1, 0.0, pltpu.roll(w[0], LANES - 1, 1)))
    before = jnp.where(lane == 0, w[0], pltpu.roll(q[-1], 1, 1))
    return [q[j] + (q[j - 1] if j else before) for j in range(tiles)]


def weighted(table, cells, k, i, j):
    index = cells[cell(i, j)]
    return (
        jnp.take_along_axis(table[k, 0], index, axis=1),
        jnp.take_along_axis(table[k, 1], index, axis=1),
    )


def advance(src, other, total, cells, table, k, tiles, first=False, mac=False):
    edges = [rim(src, plane, tiles) for plane in range(2)]
    above = [e[1] for e in edges]
    present = [e[2] for e in edges]
    for i in range(SUB):
        new, old = [], []
        for plane in range(2):
            if i < SUB - 1:
                below = [src[(plane,) + cell(i + 1, j)] for j in range(tiles)]
                pairs = [present[plane][j] + below[j] for j in range(tiles)]
            else:
                below = None
                pairs = edges[plane][0]
            h = across([pairs[j] + above[plane][j] for j in range(tiles)])
            above[plane] = pairs
            out = []
            for j in range(tiles):
                at = (plane,) + cell(i, j)
                v = present[plane][j]
                u = v - 0.125 * h[j] if first else (v + v) - (0.25 * h[j] + other[at])
                other[at] = u
                out.append(u)
            old.append(present[plane])
            present[plane] = below
            new.append(out)
        if mac:
            for j in range(tiles):
                c0r, c0i = weighted(table, cells, k, i, j)
                c1r, c1i = weighted(table, cells, k + 1, i, j)
                ur, ui = new[0][j], new[1][j]
                vr, vi = old[0][j], old[1][j]
                a = (c1r * ur - c1i * ui) + (c0r * vr - c0i * vi)
                b = (c1r * ui + c1i * ur) + (c0r * vi + c0i * vr)
                re, im = (0,) + cell(i, j), (1,) + cell(i, j)
                if first:
                    total[re], total[im] = a, b
                else:
                    total[re] = total[re] + a
                    total[im] = total[im] + b


def one_level(src, even, odd, total, cells, table, tiles):
    advance(src, odd, total, cells, table, 0, tiles, first=True, mac=True)
    for plane in range(2):
        for i in range(SUB):
            for j in range(tiles):
                even[(plane,) + cell(i, j)] = src[(plane,) + cell(i, j)]

    def pair(t, carry):
        k = 2 * t + 1
        advance(odd, even, total, cells, table, k, tiles)
        advance(even, odd, total, cells, table, k + 1, tiles, mac=True)
        return carry

    lax.fori_loop(0, ORDER // 2 - 1, pair, 0)
    advance(odd, even, total, cells, table, ORDER - 1, tiles)
    for i in range(SUB):
        for j in range(tiles):
            cr, ci = weighted(table, cells, ORDER, i, j)
            re, im = (0,) + cell(i, j), (1,) + cell(i, j)
            ur, ui = even[re], even[im]
            total[re] = total[re] + (cr * ur - ci * ui)
            total[im] = total[im] + (cr * ui + ci * ur)


def fold(block, turned, tiles):
    for j in range(tiles):
        turned[column(j), :] = block[:, column(j)].T
    return [turned[pl.ds(j, LANES, stride=tiles), :].T for j in range(tiles)]


def unfold(block, turned, tiles):
    for j in range(tiles):
        turned[pl.ds(j, LANES, stride=tiles), :] = block[:, column(j)].T
    return [turned[column(j), :].T for j in range(tiles)]


def cells_kernel(lane_ref, own, two, one, three, cells, natural, block, turned):
    here = lane_ref[0]
    tiles = cells.shape[1]
    rows = own.shape[1]
    strips = (here ^ 2, here, here ^ 3, here ^ 1)
    for piece, strip in zip((own, two, one, three), strips):
        at = pl.ds(pl.multiple_of(strip * rows, rows), rows)
        for level in range(LEVELS):
            for j in range(tiles):
                natural[level, j, at, :] = piece[level, :, column(j)]
    for level in range(LEVELS):
        for i in range(SUB):
            for j in range(tiles):
                block[pl.ds(64 * level + SUB * i, SUB), column(j)] = natural[
                    level, j, pl.ds(i, SUB, stride=SUB), :
                ].astype(jnp.float32)
    for j, tile in enumerate(fold(block, turned, tiles)):
        for level in range(LEVELS):
            cells[level, j] = tile[64 * level : 64 * level + 64].astype(jnp.int32)


def paired_cells_kernel(lane_ref, own, two, pair, *refs):
    cells_kernel(lane_ref, own, two, pair.at[0], pair.at[1], *refs)


def rows_out(level_total, bottom, natural, outs, here, rows):
    for j in range(bottom.shape[1]):
        for g in range(SUB):
            at = pl.ds(SUB * g, SUB)
            natural[0, j, at, :] = level_total[0, j, pl.ds(g, SUB, stride=SUB), :]
            natural[1, j, at, :] = bottom[0, j, pl.ds(g, SUB, stride=SUB), :]
            natural[2, j, at, :] = bottom[1, j, pl.ds(g, SUB, stride=SUB), :]
    for r, out in enumerate(outs):
        at = pl.ds(pl.multiple_of((here ^ r ^ 2) * rows, rows), rows)
        for plane in range(3):
            for j in range(bottom.shape[1]):
                out[plane, :, column(j)] = natural[plane, j, at, :]


def upper_kernel(
    lane_ref, w0, w1, w2, w3, cells, table, bottom, o0, o1, o2, o3,
    first, even, odd, block, turned, natural,
):
    here = lane_ref[0]
    rows = w0.shape[1]
    tiles = w0.shape[2] // LANES
    for r, piece in enumerate((w0, w1, w2, w3)):
        at = pl.ds(pl.multiple_of((here ^ r ^ 2) * rows, rows), rows)
        for plane in range(2):
            for j in range(tiles):
                natural[plane, j, at, :] = piece[plane, :, column(j)]
    for plane in range(2):
        for i in range(SUB):
            for j in range(tiles):
                block[pl.ds(64 * plane + SUB * i, SUB), column(j)] = natural[
                    plane, j, pl.ds(i, SUB, stride=SUB), :
                ]
    for j, tile in enumerate(fold(block, turned, tiles)):
        for plane in range(2):
            bottom[plane, j] = tile[64 * plane : 64 * plane + 64]
    one_level(bottom, even, odd, first, cells.at[0], table, tiles)
    one_level(first, even, odd, bottom, cells.at[1], table, tiles)
    rows_out(first, bottom, natural, (o0, o1, o2, o3), here, rows)


def lower_kernel(lane_ref, wave, cells, table, o0, o1, o2, o3, first, second, even, odd, natural):
    here = lane_ref[0]
    tiles = wave.shape[1]
    one_level(wave, even, odd, first, cells.at[0], table, tiles)
    one_level(first, even, odd, second, cells.at[1], table, tiles)
    rows_out(first, second, natural, (o0, o1, o2, o3), here, o0.shape[1])


def image_kernel(lane_ref, m0, m1, m2, m3, n0, n1, n2, n3, raw, squares, turned, picture):
    top = lane_ref[1] == 0
    rows = m0.shape[1]
    tiles = m0.shape[2] // LANES
    sums = []
    for level in range(LEVELS):
        early = (n0[level] + n1[level]) + (n2[level] + n3[level])
        late = (m0[level] + m1[level]) + (m2[level] + m3[level])
        total = jnp.where(top, early, early + late)
        picture[pl.ds(rows * level, rows), :] = total
        sums.append(jnp.sum(total * total))
    lane = lax.broadcasted_iota(jnp.int32, (SUB, LANES), 1)
    squares[...] = jnp.where(lane == 0, sums[0], jnp.where(lane == 1, sums[1], 0.0))
    for level in range(LEVELS):
        raw[level] = picture[pl.ds(rows * level, rows), :]


def handed_kernel(
    lane_ref, m0, m1, m2, m3, n0, n1, n2, n3, raw, handed, image, block, turned, picture
):
    here, top = lane_ref[0], lane_ref[1] == 0
    rows = m0.shape[1]
    tiles = m0.shape[2] // LANES
    for r, (m, n) in enumerate(zip((m0, m1, m2, m3), (n0, n1, n2, n3))):
        at = (here ^ r) * (2 * rows)
        for plane in range(2):
            block[pl.ds(pl.multiple_of(at + plane * rows, rows), rows), :] = jnp.where(
                top, n[1 + plane], m[1 + plane]
            )
    for j, tile in enumerate(unfold(block, turned, tiles)):
        for f in range(NFREQ):
            for plane in range(2):
                start = (2 * f + plane) * rows
                handed[f, plane, :, column(j)] = tile[start : start + rows]
    for level in range(LEVELS):
        picture[pl.ds(rows * level, rows), :] = raw[level]
    for j, tile in enumerate(unfold(picture, turned, tiles)):
        for level in range(LEVELS):
            image[level, :, column(j)] = tile[rows * level : rows * level + rows]


def call(kernel, outs, scratch, operands, moved=0):
    vmem = pl.BlockSpec(memory_space=pltpu.VMEM)
    smem = pl.BlockSpec(memory_space=pltpu.SMEM)
    return pl.pallas_call(
        kernel,
        out_shape=outs,
        in_specs=[smem] + [vmem] * (len(operands) - 1),
        out_specs=[vmem] * len(outs),
        scratch_shapes=scratch,
        compiler_params=pltpu.CompilerParams(vmem_limit_bytes=40 << 20),
        cost_estimate=pl.CostEstimate(flops=moved // 4, bytes_accessed=moved, transcendentals=0),
    )(*operands)


def frequency_shards(
    incoming_wave,
    speed_class_map,
    spectral_entry_index,
    filter_weights,
    scaled_pulsations,
    inverse_speed_classes,
):
    devices = lax.axis_size("strip")
    rows, columns = incoming_wave.shape[2], incoming_wave.shape[3]
    me = lax.axis_index("strip")
    plane, here = me // NFREQ, me % NFREQ
    planes = devices // NFREQ

    def place(p, lane):
        return (p % planes) * NFREQ + lane

    everyone = [(p, lane) for p in range(planes) for lane in range(NFREQ)]

    def send(value, pairs):
        return lax.ppermute(value, "strip", pairs)

    def in_plane(r):
        return [(place(p, n), place(p, n ^ r)) for p, n in everyone]

    def shifted(r):
        return [(place(p, n), place(p + n // 2, n ^ r)) for p, n in everyone]

    far = send(
        speed_class_map,
        [(place(p, lane), place(p + (1 if lane >= 2 else -1), lane)) for p, lane in everyone],
    )
    waves = [lax.dynamic_index_in_dim(incoming_wave, here ^ r, 0, keepdims=False) for r in range(NFREQ)]
    starts = [send(waves[r], shifted(r)) for r in (0, 1)]
    upper_half = here >= 2
    upper = jnp.where(upper_half, far, speed_class_map)
    lower = jnp.where(upper_half, speed_class_map, far)
    upper, spectral_entry_index, *crossing = lax.optimization_barrier(
        (upper, spectral_entry_index, waves[2], waves[3])
    )
    across_chip = send(upper, in_plane(2))
    starts += [send(v, shifted(r)) for r, v in zip((2, 3), crossing)]
    lanes = jnp.stack([here, (plane - jnp.where(upper_half, 0, 1)) % planes]).astype(jnp.int32)
    shape = jax.ShapeDtypeStruct
    field = (2, columns // LANES, SUB * SUB, LANES)
    half = pltpu.VMEM(field, jnp.float32)
    natural = pltpu.VMEM((3,) + field[1:], jnp.float32)
    turned = pltpu.VMEM((columns, LANES), jnp.float32)
    block = pltpu.VMEM((LANES, columns), jnp.float32)
    message = shape((3, rows, columns), jnp.float32)
    field_bytes = 4 * 2 * SUB * SUB * columns

    def folded_cells(kernel, *pieces):
        return call(
            kernel,
            [shape((LEVELS,) + field[1:], jnp.int32)],
            [pltpu.VMEM((LEVELS,) + field[1:], jnp.int32), block, turned],
            (lanes, *pieces),
            4 * field_bytes,
        )[0]

    section = (plane - 1) % planes
    entry = spectral_entry_index[section, here]
    weights = lax.dynamic_index_in_dim(filter_weights, entry, 0, keepdims=False)
    pulsation = scaled_pulsations[entry]
    angle = pulsation * inverse_speed_classes
    cosine, sine = jnp.cos(angle)[:, None], jnp.sin(angle)[:, None]
    sign = 1.0 - 2.0 * (jnp.arange(ORDER + 1) % 2).astype(jnp.float32)
    real = (weights[:, 0] * cosine - weights[:, 1] * sine) * sign
    imag = (weights[:, 0] * sine + weights[:, 1] * cosine) * sign
    table = jnp.stack([real, imag], axis=0).transpose(2, 0, 1)
    table = jnp.pad(table, ((0, 0), (0, 0), (0, LANES - NBIN)))
    table = jnp.broadcast_to(table[:, :, None, :], (ORDER + 1, 2, SUB, LANES))

    core_pair = send(jnp.stack([upper, across_chip]), in_plane(1))
    upper_cells = folded_cells(paired_cells_kernel, upper, across_chip, core_pair)
    lower, upper_cells = lax.optimization_barrier((lower, upper_cells))
    lower_pieces = [lower] + [send(lower, in_plane(r)) for r in (2, 1, 3)]
    bottom, *early = call(
        upper_kernel,
        [shape(field, jnp.float32)] + [message] * NFREQ,
        [half, half, half, block, turned, natural],
        (lanes, *starts, upper_cells, table),
        80 * field_bytes,
    )
    early, lower_pieces = lax.optimization_barrier((early, lower_pieces))
    early = [
        send(v, [(place(p, n), place(p - (n ^ r) // 2, n ^ r)) for p, n in everyone])
        for r, v in enumerate(early)
    ]
    lower_cells = folded_cells(cells_kernel, *lower_pieces)
    late = call(
        lower_kernel,
        [message] * NFREQ,
        [half, half, half, half, natural],
        (lanes, bottom, lower_cells, table),
        80 * field_bytes,
    )
    late, early = lax.optimization_barrier((late, early))
    late = [
        send(v, [(place(p, n), place(p + 1 - (n ^ r) // 2, n ^ r)) for p, n in everyone])
        for r, v in enumerate(late)
    ]
    raw, squares = call(
        image_kernel,
        [shape(speed_class_map.shape, jnp.float32), shape((SUB, LANES), jnp.float32)],
        [turned, block],
        (lanes, *late, *early),
        2 * field_bytes,
    )
    handed, raw = call(
        handed_kernel,
        [shape(incoming_wave.shape, jnp.float32), shape(speed_class_map.shape, jnp.float32)],
        [block, turned, block],
        (lanes, *late, *early, raw),
        8 * field_bytes,
    )

    def owner(s, strip):
        return place(s + strip // 2, strip ^ 2)

    mean_square = squares
    for r in range(1, NFREQ):
        mean_square = mean_square + send(
            squares,
            [(owner(s, strip), owner(s, strip ^ r)) for s in range(planes) for strip in range(NFREQ)],
        )
    mean_square = mean_square[0, :LEVELS] / (rows * NFREQ * columns)
    image = raw / jnp.sqrt(mean_square + 1e-06)[:, None, None]
    return (image, handed)


def shards(*operands):
    lateral_count = lax.axis_size("strip") // SECTIONS
    rows, columns = operands[0].shape[2:]
    if lateral_count == NFREQ and rows * lateral_count == SUB * SUB and columns == SUB * LANES:
        return frequency_shards(*operands)
    return strip_shards(*operands)


def solution(mesh):
    return jax.shard_map(
        shards,
        mesh=mesh,
        in_specs=(
            P("groups", None, "strip", None),
            P("groups", "strip", None),
            P("groups", None),
            P(),
            P(),
            P(),
        ),
        out_specs=(P("groups", "strip", None), P("groups", None, "strip", None)),
        check_vma=False,
    )
```

```python
import functools

import jax
import jax.numpy as jnp
from jax import lax
from jax.experimental import pallas as pl
from jax.experimental.pallas import tpu as pltpu
from jax.sharding import PartitionSpec as P

SECTIONS = 4
LEVELS = 2
ORDER = 12
NFREQ = 4
NBIN = 16
NW = 16


def extended_2(shard, sides, width):
    for axis, dim in sides:
        devices, length = (lax.axis_size(axis), shard.shape[dim])
        up = [(i, (i + 1) % devices) for i in range(devices)]
        down = [(j, i) for i, j in up]
        last = lax.slice_in_dim(shard, length - width, length, axis=dim)
        initial = lax.slice_in_dim(shard, 0, width, axis=dim)
        before = lax.ppermute(last, axis, up)
        after = lax.ppermute(initial, axis, down)
        shard = jnp.concatenate([before, shard, after], axis=dim)
    return shard


def from_behind(shard, axis, by):
    devices = lax.axis_size(axis)
    return lax.ppermute(shard, axis, [(i, (i + by) % devices) for i in range(devices)])


def stencil_padded(padded):
    vertical = padded[:, :, :-2, :] + padded[:, :, 2:, :]
    middle = padded[:, :, 1:-1, :]
    return (
        -0.5 * middle[..., 1:-1]
        + 0.25 * (vertical[..., 1:-1] + middle[..., :-2] + middle[..., 2:])
        + 0.125 * (vertical[..., :-2] + vertical[..., 2:])
    )


def complex_times(coeff, field):
    real_part = coeff[:, 0] * field[:, 0] - coeff[:, 1] * field[:, 1]
    imag_part = coeff[:, 0] * field[:, 1] + coeff[:, 1] * field[:, 0]
    return jnp.stack([real_part, imag_part], axis=1)


def strip_shards(
    incoming_wave,
    speed_class_map,
    spectral_entry_index,
    filter_weights,
    scaled_pulsations,
    inverse_speed_classes,
):
    highest = lax.Precision.HIGHEST
    summed_along = incoming_wave.shape[2]
    summed_across = incoming_wave.shape[3]
    strip_count = lax.axis_size("strip")
    lateral_count = strip_count // SECTIONS
    position = (lax.axis_index("strip") - lateral_count // 2) % strip_count
    vertical_slab = position // lateral_count
    lateral_place = position % lateral_count
    section_rows = summed_along * lateral_count
    section_cells = section_rows * summed_across
    margin = ORDER
    extended_rows = summed_along + 2 * margin
    lateral_rows = (
        lateral_place * summed_along - margin + jnp.arange(extended_rows, dtype=jnp.int32)
    )
    inside = ((lateral_rows >= 0) & (lateral_rows < section_rows)).astype(jnp.float32)[
        None, None, :, None
    ]

    def mcclellan_step(field):
        padded = jnp.pad(field, ((0, 0), (0, 0), (1, 1), (0, 0)))
        padded = jnp.pad(padded, ((0, 0), (0, 0), (0, 0), (1, 1)))
        result = stencil_padded(padded)
        result = result * inside
        return result

    def interior(field):
        return field[:, :, margin : margin + summed_along, :]

    def image_downward(field, batch_index):
        freq_row = lax.dynamic_index_in_dim(spectral_entry_index, batch_index, 0, keepdims=False)
        freq_select = (freq_row[:, None] == jnp.arange(NW, dtype=jnp.int32)[None, :]).astype(
            jnp.float32
        )
        freq_coeffs = jnp.einsum("fw,wbck->fbck", freq_select, filter_weights, precision=highest)
        freq_omega = jnp.dot(freq_select, scaled_pulsations, precision=highest)
        wavefield = field
        raws = []
        for level in range(LEVELS):
            cells = speed_class_map[level].reshape(-1)
            bin_onehot = (cells[None, :] == jnp.arange(NBIN, dtype=jnp.int32)[:, None]).astype(
                jnp.float32
            )
            cell_slowness = jnp.dot(inverse_speed_classes, bin_onehot, precision=highest).reshape(
                summed_along, summed_across
            )
            table = jnp.einsum("fbck,bn->kfcn", freq_coeffs, bin_onehot, precision=highest).reshape(
                ORDER + 1, NFREQ, 2, summed_along, summed_across
            )
            extended = extended_2(wavefield, (("strip", 2),), ORDER) * inside
            previous = extended
            current = mcclellan_step(extended)
            accumulated = complex_times(table[0], interior(previous)) + complex_times(
                table[1], interior(current)
            )

            def recursion_step(order_index, state_tuple):
                before, present, running = state_tuple
                following = 2.0 * mcclellan_step(present) - before
                coeff = lax.dynamic_index_in_dim(table, order_index, 0, keepdims=False)
                running = running + complex_times(coeff, interior(following))
                return (present, following, running)

            previous, current, accumulated = lax.fori_loop(
                2, ORDER + 1, recursion_step, (previous, current, accumulated)
            )
            phase_angle = freq_omega[:, None, None] * cell_slowness[None]
            cosine = jnp.cos(phase_angle)
            sine_part = jnp.sin(phase_angle)
            real_part = accumulated[:, 0] * cosine - accumulated[:, 1] * sine_part
            imag_part = accumulated[:, 0] * sine_part + accumulated[:, 1] * cosine
            wavefield = jnp.stack([real_part, imag_part], axis=1)
            raws.append(jnp.sum(real_part, axis=0))
        return (wavefield, raws)

    above_floor_lines, above_unscaled_waves = image_downward(incoming_wave, vertical_slab)
    arriving = from_behind(above_floor_lines, "strip", lateral_count)
    second_bottom, second_raws = image_downward(arriving, jnp.maximum(vertical_slab - 1, 0))
    handed = jnp.where(vertical_slab == 0, above_floor_lines, second_bottom)
    first_section = (vertical_slab > 0).astype(jnp.float32)
    totals = [
        above_unscaled_waves[level] + first_section * second_raws[level] for level in range(LEVELS)
    ]
    selector = (jnp.arange(SECTIONS, dtype=jnp.int32) == vertical_slab).astype(jnp.float32)
    images = []
    for level in range(LEVELS):
        raw_image = totals[level]
        spread = lax.psum(selector * jnp.sum(raw_image * raw_image), "strip")
        mean_square = jnp.sum(spread * selector) / section_cells
        images.append(raw_image / jnp.sqrt(mean_square + 1e-06))
    return (jnp.stack(images, axis=0), handed)


LANES = 128
SUB = 8


def cell(i, j):
    return (j, pl.ds(SUB * i, SUB), slice(None))


def column(j):
    return pl.ds(LANES * j, LANES)


def rim(src, plane, tiles):
    sub = lax.broadcasted_iota(jnp.int32, (SUB, LANES), 0)
    lower, upper, rows = [], [], []
    for j in range(tiles):
        v0 = src[(plane,) + cell(0, j)]
        v7 = src[(plane,) + cell(SUB - 1, j)]
        p = v7 + jnp.where(sub == SUB - 1, 0.0, pltpu.roll(v0, SUB - 1, 0))
        lower.append(p)
        upper.append(jnp.where(sub == 0, v0, pltpu.roll(p, 1, 0)))
        rows.append(v0)
    return lower, upper, rows


def across(w):
    lane = lax.broadcasted_iota(jnp.int32, (SUB, LANES), 1)
    tiles = len(w)
    q = [w[j] + w[j + 1] for j in range(tiles - 1)]
    q.append(w[-1] + jnp.where(lane == LANES - 1, 0.0, pltpu.roll(w[0], LANES - 1, 1)))
    before = jnp.where(lane == 0, w[0], pltpu.roll(q[-1], 1, 1))
    return [q[j] + (q[j - 1] if j else before) for j in range(tiles)]


def pick(table, index):
    numbers = lax.GatherDimensionNumbers(
        offset_dims=(),
        collapsed_slice_dims=(1,),
        start_index_map=(1,),
        operand_batching_dims=(0,),
        start_indices_batching_dims=(0,),
    )
    return lax.gather(
        table,
        index[..., None],
        numbers,
        slice_sizes=(1, 1),
        mode=lax.GatherScatterMode.PROMISE_IN_BOUNDS,
    )


def weighted(table, cells, k, i, j):
    code = pick(table[k], cells[cell(i, j)])
    return code.astype(jnp.float32), (code << 16).astype(jnp.float32)


def advance(src, other, total, cells, table, k, tiles, first=False, mac=False):
    edges = [rim(src, plane, tiles) for plane in range(2)]
    above = [e[1] for e in edges]
    present = [e[2] for e in edges]
    for i in range(SUB):
        new, old = [], []
        for plane in range(2):
            if i < SUB - 1:
                below = [src[(plane,) + cell(i + 1, j)] for j in range(tiles)]
                pairs = [present[plane][j] + below[j] for j in range(tiles)]
            else:
                below = None
                pairs = edges[plane][0]
            h = across([pairs[j] + above[plane][j] for j in range(tiles)])
            above[plane] = pairs
            out = []
            for j in range(tiles):
                at = (plane,) + cell(i, j)
                v = present[plane][j]
                u = v - 0.125 * h[j] if first else (v + v) - (0.25 * h[j] + other[at])
                other[at] = u
                out.append(u)
            old.append(present[plane])
            present[plane] = below
            new.append(out)
        if mac:
            for j in range(tiles):
                c0r, c0i = weighted(table, cells, k, i, j)
                c1r, c1i = weighted(table, cells, k + 1, i, j)
                ur, ui = new[0][j], new[1][j]
                vr, vi = old[0][j], old[1][j]
                a = (c1r * ur - c1i * ui) + (c0r * vr - c0i * vi)
                b = (c1r * ui + c1i * ur) + (c0r * vi + c0i * vr)
                re, im = (0,) + cell(i, j), (1,) + cell(i, j)
                if first:
                    total[re], total[im] = a, b
                else:
                    total[re] = total[re] + a
                    total[im] = total[im] + b


def packed(table, codes, scale):
    largest = jnp.zeros((SUB, LANES), jnp.float32)
    for k in range(ORDER + 1):
        for part in range(2):
            largest = jnp.maximum(largest, jnp.abs(table[k, part]))
    largest = jnp.where(largest > 0, largest, 1.0)
    for k in range(ORDER + 1):
        low = jnp.round(table[k, 1] / largest * 32767.0)
        high = jnp.round(table[k, 0] / largest * 32767.0 - low / 65536.0)
        codes[k] = high.astype(jnp.int32) * 65536 + low.astype(jnp.int32)
    scale[...] = largest / (32767.0 * 65536.0)


def one_level(src, even, odd, total, cells, table, scale, tiles):
    advance(src, odd, total, cells, table, 0, tiles, first=True, mac=True)
    for plane in range(2):
        for i in range(SUB):
            for j in range(tiles):
                even[(plane,) + cell(i, j)] = src[(plane,) + cell(i, j)]

    def pair(t, carry):
        k = 2 * t + 1
        advance(odd, even, total, cells, table, k, tiles)
        advance(even, odd, total, cells, table, k + 1, tiles, mac=True)
        return carry

    lax.fori_loop(0, ORDER // 2 - 1, pair, 0)
    advance(odd, even, total, cells, table, ORDER - 1, tiles)
    for i in range(SUB):
        for j in range(tiles):
            cr, ci = weighted(table, cells, ORDER, i, j)
            re, im = (0,) + cell(i, j), (1,) + cell(i, j)
            ur, ui = even[re], even[im]
            unit = pick(scale[...], cells[cell(i, j)])
            total[re] = (total[re] + (cr * ur - ci * ui)) * unit
            total[im] = (total[im] + (cr * ui + ci * ur)) * unit


def fold(block, turned, tiles):
    for j in range(tiles):
        turned[column(j), :] = block[:, column(j)].T
    return [turned[pl.ds(j, LANES, stride=tiles), :].T for j in range(tiles)]


def unfold(block, turned, tiles):
    for j in range(tiles):
        turned[pl.ds(j, LANES, stride=tiles), :] = block[:, column(j)].T
    return [turned[column(j), :].T for j in range(tiles)]


def cells_kernel(lane_ref, own, two, one, three, cells, natural, block, turned):
    here = lane_ref[0]
    tiles = cells.shape[1]
    rows = own.shape[1]
    strips = (here ^ 2, here, here ^ 3, here ^ 1)
    for piece, strip in zip((own, two, one, three), strips):
        at = pl.ds(pl.multiple_of(strip * rows, rows), rows)
        for level in range(LEVELS):
            for j in range(tiles):
                natural[level, j, at, :] = piece[level, :, column(j)]
    for level in range(LEVELS):
        for i in range(SUB):
            for j in range(tiles):
                block[pl.ds(64 * level + SUB * i, SUB), column(j)] = natural[
                    level, j, pl.ds(i, SUB, stride=SUB), :
                ].astype(jnp.float32)
    for j, tile in enumerate(fold(block, turned, tiles)):
        for level in range(LEVELS):
            cells[level, j] = tile[64 * level : 64 * level + 64].astype(jnp.int32)


def paired_cells_kernel(lane_ref, own, two, pair, *refs):
    cells_kernel(lane_ref, own, two, pair.at[0], pair.at[1], *refs)


def rows_out(level_total, bottom, natural, outs, here, rows):
    for j in range(bottom.shape[1]):
        for g in range(SUB):
            at = pl.ds(SUB * g, SUB)
            natural[0, j, at, :] = level_total[0, j, pl.ds(g, SUB, stride=SUB), :]
            natural[1, j, at, :] = bottom[0, j, pl.ds(g, SUB, stride=SUB), :]
            natural[2, j, at, :] = bottom[1, j, pl.ds(g, SUB, stride=SUB), :]
    for r, out in enumerate(outs):
        at = pl.ds(pl.multiple_of((here ^ r ^ 2) * rows, rows), rows)
        for plane in range(3):
            for j in range(bottom.shape[1]):
                out[plane, :, column(j)] = natural[plane, j, at, :]


def upper_kernel(
    lane_ref, w0, w1, w2, w3, cells, table, bottom, o0, o1, o2, o3,
    first, even, odd, block, turned, natural, codes, scale,
):
    here = lane_ref[0]
    rows = w0.shape[1]
    tiles = w0.shape[2] // LANES
    for r, piece in enumerate((w0, w1, w2, w3)):
        at = pl.ds(pl.multiple_of((here ^ r ^ 2) * rows, rows), rows)
        for plane in range(2):
            for j in range(tiles):
                natural[plane, j, at, :] = piece[plane, :, column(j)]
    for plane in range(2):
        for i in range(SUB):
            for j in range(tiles):
                block[pl.ds(64 * plane + SUB * i, SUB), column(j)] = natural[
                    plane, j, pl.ds(i, SUB, stride=SUB), :
                ]
    for j, tile in enumerate(fold(block, turned, tiles)):
        for plane in range(2):
            bottom[plane, j] = tile[64 * plane : 64 * plane + 64]
    packed(table, codes, scale)
    one_level(bottom, even, odd, first, cells.at[0], codes, scale, tiles)
    one_level(first, even, odd, bottom, cells.at[1], codes, scale, tiles)
    rows_out(first, bottom, natural, (o0, o1, o2, o3), here, rows)


def lower_kernel(
    lane_ref, wave, cells, table, o0, o1, o2, o3, first, second, even, odd, natural, codes, scale
):
    here = lane_ref[0]
    tiles = wave.shape[1]
    packed(table, codes, scale)
    one_level(wave, even, odd, first, cells.at[0], codes, scale, tiles)
    one_level(first, even, odd, second, cells.at[1], codes, scale, tiles)
    rows_out(first, second, natural, (o0, o1, o2, o3), here, o0.shape[1])


def image_kernel(lane_ref, m0, m1, m2, m3, n0, n1, n2, n3, raw, squares, turned, picture):
    top = lane_ref[1] == 0
    rows = m0.shape[1]
    tiles = m0.shape[2] // LANES
    sums = []
    for level in range(LEVELS):
        early = (n0[level] + n1[level]) + (n2[level] + n3[level])
        late = (m0[level] + m1[level]) + (m2[level] + m3[level])
        total = jnp.where(top, early, early + late)
        picture[pl.ds(rows * level, rows), :] = total
        sums.append(jnp.sum(total * total))
    lane = lax.broadcasted_iota(jnp.int32, (SUB, LANES), 1)
    squares[...] = jnp.where(lane == 0, sums[0], jnp.where(lane == 1, sums[1], 0.0))
    for level in range(LEVELS):
        raw[level] = picture[pl.ds(rows * level, rows), :]


def handed_kernel(
    lane_ref, m0, m1, m2, m3, n0, n1, n2, n3, raw, handed, image, block, turned, picture
):
    here, top = lane_ref[0], lane_ref[1] == 0
    rows = m0.shape[1]
    tiles = m0.shape[2] // LANES
    for r, (m, n) in enumerate(zip((m0, m1, m2, m3), (n0, n1, n2, n3))):
        at = (here ^ r) * (2 * rows)
        for plane in range(2):
            block[pl.ds(pl.multiple_of(at + plane * rows, rows), rows), :] = jnp.where(
                top, n[1 + plane], m[1 + plane]
            )
    for j, tile in enumerate(unfold(block, turned, tiles)):
        for f in range(NFREQ):
            for plane in range(2):
                start = (2 * f + plane) * rows
                handed[f, plane, :, column(j)] = tile[start : start + rows]
    for level in range(LEVELS):
        picture[pl.ds(rows * level, rows), :] = raw[level]
    for j, tile in enumerate(unfold(picture, turned, tiles)):
        for level in range(LEVELS):
            image[level, :, column(j)] = tile[rows * level : rows * level + rows]


def call(kernel, outs, scratch, operands, moved=0):
    vmem = pl.BlockSpec(memory_space=pltpu.VMEM)
    smem = pl.BlockSpec(memory_space=pltpu.SMEM)
    return pl.pallas_call(
        kernel,
        out_shape=outs,
        in_specs=[smem] + [vmem] * (len(operands) - 1),
        out_specs=[vmem] * len(outs),
        scratch_shapes=scratch,
        compiler_params=pltpu.CompilerParams(vmem_limit_bytes=40 << 20),
        cost_estimate=pl.CostEstimate(flops=moved // 4, bytes_accessed=moved, transcendentals=0),
    )(*operands)


def frequency_shards(
    incoming_wave,
    speed_class_map,
    spectral_entry_index,
    filter_weights,
    scaled_pulsations,
    inverse_speed_classes,
):
    devices = lax.axis_size("strip")
    rows, columns = incoming_wave.shape[2], incoming_wave.shape[3]
    me = lax.axis_index("strip")
    plane, here = me // NFREQ, me % NFREQ
    planes = devices // NFREQ

    def place(p, lane):
        return (p % planes) * NFREQ + lane

    everyone = [(p, lane) for p in range(planes) for lane in range(NFREQ)]

    def send(value, pairs):
        return lax.ppermute(value, "strip", pairs)

    def in_plane(r):
        return [(place(p, n), place(p, n ^ r)) for p, n in everyone]

    def shifted(r):
        return [(place(p, n), place(p + n // 2, n ^ r)) for p, n in everyone]

    far = send(
        speed_class_map,
        [(place(p, lane), place(p + (1 if lane >= 2 else -1), lane)) for p, lane in everyone],
    )
    waves = [lax.dynamic_index_in_dim(incoming_wave, here ^ r, 0, keepdims=False) for r in range(NFREQ)]
    starts = [send(waves[r], shifted(r)) for r in (0, 1)]
    upper_half = here >= 2
    upper = jnp.where(upper_half, far, speed_class_map)
    lower = jnp.where(upper_half, speed_class_map, far)
    upper, spectral_entry_index, *crossing = lax.optimization_barrier(
        (upper, spectral_entry_index, waves[2], waves[3])
    )
    across_chip = send(upper, in_plane(2))
    starts += [send(v, shifted(r)) for r, v in zip((2, 3), crossing)]
    lanes = jnp.stack([here, (plane - jnp.where(upper_half, 0, 1)) % planes]).astype(jnp.int32)
    shape = jax.ShapeDtypeStruct
    field = (2, columns // LANES, SUB * SUB, LANES)
    half = pltpu.VMEM(field, jnp.float32)
    natural = pltpu.VMEM((3,) + field[1:], jnp.float32)
    turned = pltpu.VMEM((columns, LANES), jnp.float32)
    block = pltpu.VMEM((LANES, columns), jnp.float32)
    codes = pltpu.VMEM((ORDER + 1, SUB, LANES), jnp.int32)
    scale = pltpu.VMEM((SUB, LANES), jnp.float32)
    message = shape((3, rows, columns), jnp.float32)
    field_bytes = 4 * 2 * SUB * SUB * columns

    def folded_cells(kernel, *pieces):
        return call(
            kernel,
            [shape((LEVELS,) + field[1:], jnp.int32)],
            [pltpu.VMEM((LEVELS,) + field[1:], jnp.int32), block, turned],
            (lanes, *pieces),
            4 * field_bytes,
        )[0]

    section = (plane - 1) % planes
    entry = spectral_entry_index[section, here]
    weights = lax.dynamic_index_in_dim(filter_weights, entry, 0, keepdims=False)
    pulsation = scaled_pulsations[entry]
    angle = pulsation * inverse_speed_classes
    cosine, sine = jnp.cos(angle)[:, None], jnp.sin(angle)[:, None]
    sign = 1.0 - 2.0 * (jnp.arange(ORDER + 1) % 2).astype(jnp.float32)
    real = (weights[:, 0] * cosine - weights[:, 1] * sine) * sign
    imag = (weights[:, 0] * sine + weights[:, 1] * cosine) * sign
    table = jnp.stack([real, imag], axis=0).transpose(2, 0, 1)
    table = jnp.pad(table, ((0, 0), (0, 0), (0, LANES - NBIN)))
    table = jnp.broadcast_to(table[:, :, None, :], (ORDER + 1, 2, SUB, LANES))
    core_pair = send(jnp.stack([upper, across_chip]), in_plane(1))
    upper_cells = folded_cells(paired_cells_kernel, upper, across_chip, core_pair)
    lower, upper_cells = lax.optimization_barrier((lower, upper_cells))
    lower_pieces = [lower] + [send(lower, in_plane(r)) for r in (2, 1, 3)]
    bottom, *early = call(
        upper_kernel,
        [shape(field, jnp.float32)] + [message] * NFREQ,
        [half, half, half, block, turned, natural, codes, scale],
        (lanes, *starts, upper_cells, table),
        80 * field_bytes,
    )
    early, lower_pieces = lax.optimization_barrier((early, lower_pieces))
    early = [
        send(v, [(place(p, n), place(p - (n ^ r) // 2, n ^ r)) for p, n in everyone])
        for r, v in enumerate(early)
    ]
    lower_cells = folded_cells(cells_kernel, *lower_pieces)
    late = call(
        lower_kernel,
        [message] * NFREQ,
        [half, half, half, half, natural, codes, scale],
        (lanes, bottom, lower_cells, table),
        80 * field_bytes,
    )
    late, early = lax.optimization_barrier((late, early))
    late = [
        send(v, [(place(p, n), place(p + 1 - (n ^ r) // 2, n ^ r)) for p, n in everyone])
        for r, v in enumerate(late)
    ]
    raw, squares = call(
        image_kernel,
        [shape(speed_class_map.shape, jnp.float32), shape((SUB, LANES), jnp.float32)],
        [turned, block],
        (lanes, *late, *early),
        2 * field_bytes,
    )
    handed, raw = call(
        handed_kernel,
        [shape(incoming_wave.shape, jnp.float32), shape(speed_class_map.shape, jnp.float32)],
        [block, turned, block],
        (lanes, *late, *early, raw),
        8 * field_bytes,
    )

    def owner(s, strip):
        return place(s + strip // 2, strip ^ 2)

    mean_square = squares
    for r in range(1, NFREQ):
        mean_square = mean_square + send(
            squares,
            [(owner(s, strip), owner(s, strip ^ r)) for s in range(planes) for strip in range(NFREQ)],
        )
    mean_square = mean_square[0, :LEVELS] / (rows * NFREQ * columns)
    image = raw / jnp.sqrt(mean_square + 1e-06)[:, None, None]
    return (image, handed)


def shards(*operands):
    lateral_count = lax.axis_size("strip") // SECTIONS
    rows, columns = operands[0].shape[2:]
    if lateral_count == NFREQ and rows * lateral_count == SUB * SUB and columns == SUB * LANES:
        return frequency_shards(*operands)
    return strip_shards(*operands)


def solution(mesh):
    return jax.shard_map(
        shards,
        mesh=mesh,
        in_specs=(
            P("groups", None, "strip", None),
            P("groups", "strip", None),
            P("groups", None),
            P(),
            P(),
            P(),
        ),
        out_specs=(P("groups", "strip", None), P("groups", None, "strip", None)),
        check_vma=False,
    )
```

```python
import functools

import jax
import jax.numpy as jnp
from jax import lax
from jax.experimental import pallas as pl
from jax.experimental.pallas import tpu as pltpu
from jax.sharding import PartitionSpec as P

SECTIONS = 4
LEVELS = 2
ORDER = 12
NFREQ = 4
NBIN = 16
NW = 16


def extended_2(shard, sides, width):
    for axis, dim in sides:
        devices, length = (lax.axis_size(axis), shard.shape[dim])
        up = [(i, (i + 1) % devices) for i in range(devices)]
        down = [(j, i) for i, j in up]
        last = lax.slice_in_dim(shard, length - width, length, axis=dim)
        initial = lax.slice_in_dim(shard, 0, width, axis=dim)
        before = lax.ppermute(last, axis, up)
        after = lax.ppermute(initial, axis, down)
        shard = jnp.concatenate([before, shard, after], axis=dim)
    return shard


def from_behind(shard, axis, by):
    devices = lax.axis_size(axis)
    return lax.ppermute(shard, axis, [(i, (i + by) % devices) for i in range(devices)])


def stencil_padded(padded):
    vertical = padded[:, :, :-2, :] + padded[:, :, 2:, :]
    middle = padded[:, :, 1:-1, :]
    return (
        -0.5 * middle[..., 1:-1]
        + 0.25 * (vertical[..., 1:-1] + middle[..., :-2] + middle[..., 2:])
        + 0.125 * (vertical[..., :-2] + vertical[..., 2:])
    )


def complex_times(coeff, field):
    real_part = coeff[:, 0] * field[:, 0] - coeff[:, 1] * field[:, 1]
    imag_part = coeff[:, 0] * field[:, 1] + coeff[:, 1] * field[:, 0]
    return jnp.stack([real_part, imag_part], axis=1)


def strip_shards(
    incoming_wave,
    speed_class_map,
    spectral_entry_index,
    filter_weights,
    scaled_pulsations,
    inverse_speed_classes,
):
    highest = lax.Precision.HIGHEST
    summed_along = incoming_wave.shape[2]
    summed_across = incoming_wave.shape[3]
    strip_count = lax.axis_size("strip")
    lateral_count = strip_count // SECTIONS
    position = (lax.axis_index("strip") - lateral_count // 2) % strip_count
    vertical_slab = position // lateral_count
    lateral_place = position % lateral_count
    section_rows = summed_along * lateral_count
    section_cells = section_rows * summed_across
    margin = ORDER
    extended_rows = summed_along + 2 * margin
    lateral_rows = (
        lateral_place * summed_along - margin + jnp.arange(extended_rows, dtype=jnp.int32)
    )
    inside = ((lateral_rows >= 0) & (lateral_rows < section_rows)).astype(jnp.float32)[
        None, None, :, None
    ]

    def mcclellan_step(field):
        padded = jnp.pad(field, ((0, 0), (0, 0), (1, 1), (0, 0)))
        padded = jnp.pad(padded, ((0, 0), (0, 0), (0, 0), (1, 1)))
        result = stencil_padded(padded)
        result = result * inside
        return result

    def interior(field):
        return field[:, :, margin : margin + summed_along, :]

    def image_downward(field, batch_index):
        freq_row = lax.dynamic_index_in_dim(spectral_entry_index, batch_index, 0, keepdims=False)
        freq_select = (freq_row[:, None] == jnp.arange(NW, dtype=jnp.int32)[None, :]).astype(
            jnp.float32
        )
        freq_coeffs = jnp.einsum("fw,wbck->fbck", freq_select, filter_weights, precision=highest)
        freq_omega = jnp.dot(freq_select, scaled_pulsations, precision=highest)
        wavefield = field
        raws = []
        for level in range(LEVELS):
            cells = speed_class_map[level].reshape(-1)
            bin_onehot = (cells[None, :] == jnp.arange(NBIN, dtype=jnp.int32)[:, None]).astype(
                jnp.float32
            )
            cell_slowness = jnp.dot(inverse_speed_classes, bin_onehot, precision=highest).reshape(
                summed_along, summed_across
            )
            table = jnp.einsum("fbck,bn->kfcn", freq_coeffs, bin_onehot, precision=highest).reshape(
                ORDER + 1, NFREQ, 2, summed_along, summed_across
            )
            extended = extended_2(wavefield, (("strip", 2),), ORDER) * inside
            previous = extended
            current = mcclellan_step(extended)
            accumulated = complex_times(table[0], interior(previous)) + complex_times(
                table[1], interior(current)
            )

            def recursion_step(order_index, state_tuple):
                before, present, running = state_tuple
                following = 2.0 * mcclellan_step(present) - before
                coeff = lax.dynamic_index_in_dim(table, order_index, 0, keepdims=False)
                running = running + complex_times(coeff, interior(following))
                return (present, following, running)

            previous, current, accumulated = lax.fori_loop(
                2, ORDER + 1, recursion_step, (previous, current, accumulated)
            )
            phase_angle = freq_omega[:, None, None] * cell_slowness[None]
            cosine = jnp.cos(phase_angle)
            sine_part = jnp.sin(phase_angle)
            real_part = accumulated[:, 0] * cosine - accumulated[:, 1] * sine_part
            imag_part = accumulated[:, 0] * sine_part + accumulated[:, 1] * cosine
            wavefield = jnp.stack([real_part, imag_part], axis=1)
            raws.append(jnp.sum(real_part, axis=0))
        return (wavefield, raws)

    above_floor_lines, above_unscaled_waves = image_downward(incoming_wave, vertical_slab)
    arriving = from_behind(above_floor_lines, "strip", lateral_count)
    second_bottom, second_raws = image_downward(arriving, jnp.maximum(vertical_slab - 1, 0))
    handed = jnp.where(vertical_slab == 0, above_floor_lines, second_bottom)
    first_section = (vertical_slab > 0).astype(jnp.float32)
    totals = [
        above_unscaled_waves[level] + first_section * second_raws[level] for level in range(LEVELS)
    ]
    selector = (jnp.arange(SECTIONS, dtype=jnp.int32) == vertical_slab).astype(jnp.float32)
    images = []
    for level in range(LEVELS):
        raw_image = totals[level]
        spread = lax.psum(selector * jnp.sum(raw_image * raw_image), "strip")
        mean_square = jnp.sum(spread * selector) / section_cells
        images.append(raw_image / jnp.sqrt(mean_square + 1e-06))
    return (jnp.stack(images, axis=0), handed)


LANES = 128
SUB = 8


def cell(i, j):
    return (j, pl.ds(SUB * i, SUB), slice(None))


def column(j):
    return pl.ds(LANES * j, LANES)


def rim(src, plane, tiles):
    sub = lax.broadcasted_iota(jnp.int32, (SUB, LANES), 0)
    lower, upper, rows = [], [], []
    for j in range(tiles):
        v0 = src[(plane,) + cell(0, j)]
        v7 = src[(plane,) + cell(SUB - 1, j)]
        p = v7 + jnp.where(sub == SUB - 1, 0.0, pltpu.roll(v0, SUB - 1, 0))
        lower.append(p)
        upper.append(jnp.where(sub == 0, v0, pltpu.roll(p, 1, 0)))
        rows.append(v0)
    return lower, upper, rows


def across(w):
    lane = lax.broadcasted_iota(jnp.int32, (SUB, LANES), 1)
    tiles = len(w)
    q = [w[j] + w[j + 1] for j in range(tiles - 1)]
    q.append(w[-1] + jnp.where(lane == LANES - 1, 0.0, pltpu.roll(w[0], LANES - 1, 1)))
    before = jnp.where(lane == 0, w[0], pltpu.roll(q[-1], 1, 1))
    return [q[j] + (q[j - 1] if j else before) for j in range(tiles)]


def pick(table, index):
    numbers = lax.GatherDimensionNumbers(
        offset_dims=(),
        collapsed_slice_dims=(1,),
        start_index_map=(1,),
        operand_batching_dims=(0,),
        start_indices_batching_dims=(0,),
    )
    return lax.gather(
        table,
        index[..., None],
        numbers,
        slice_sizes=(1, 1),
        mode=lax.GatherScatterMode.PROMISE_IN_BOUNDS,
    )


def weighted(table, cells, k, i, j):
    code = pick(table[k], cells[cell(i, j)])
    return code.astype(jnp.float32), (code << 16).astype(jnp.float32)


def advance(src, other, tiles, first=False):
    edges = [rim(src, plane, tiles) for plane in range(2)]
    above = [e[1] for e in edges]
    present = [e[2] for e in edges]
    for i in range(SUB):
        for plane in range(2):
            if i < SUB - 1:
                below = [src[(plane,) + cell(i + 1, j)] for j in range(tiles)]
                pairs = [present[plane][j] + below[j] for j in range(tiles)]
            else:
                below = None
                pairs = edges[plane][0]
            h = across([pairs[j] + above[plane][j] for j in range(tiles)])
            above[plane] = pairs
            for j in range(tiles):
                at = (plane,) + cell(i, j)
                v = present[plane][j]
                u = v - 0.125 * h[j] if first else (v + v) - (0.25 * h[j] + other[at])
                other[at] = u
            present[plane] = below


def add_orders(lower, upper, total, cells, table, k, tiles, first=False):
    for i in range(SUB):
        for j in range(tiles):
            c0r, c0i = weighted(table, cells, k, i, j)
            c1r, c1i = weighted(table, cells, k + 1, i, j)
            re, im = (0,) + cell(i, j), (1,) + cell(i, j)
            ur, ui = upper[re], upper[im]
            vr, vi = lower[re], lower[im]
            a = (c1r * ur - c1i * ui) + (c0r * vr - c0i * vi)
            b = (c1r * ui + c1i * ur) + (c0r * vi + c0i * vr)
            if first:
                total[re], total[im] = a, b
            else:
                total[re] = total[re] + a
                total[im] = total[im] + b


def packed(table, codes, scale):
    largest = jnp.zeros((SUB, LANES), jnp.float32)
    for k in range(ORDER + 1):
        for part in range(2):
            largest = jnp.maximum(largest, jnp.abs(table[k, part]))
    largest = jnp.where(largest > 0, largest, 1.0)
    for k in range(ORDER + 1):
        low = jnp.round(table[k, 1] / largest * 32767.0)
        high = jnp.round(table[k, 0] / largest * 32767.0 - low / 65536.0)
        codes[k] = high.astype(jnp.int32) * 65536 + low.astype(jnp.int32)
    scale[...] = largest / (32767.0 * 65536.0)


def one_level(src, even, odd, total, cells, table, scale, tiles):
    advance(src, odd, tiles, first=True)
    add_orders(src, odd, total, cells, table, 0, tiles, first=True)
    for plane in range(2):
        for i in range(SUB):
            for j in range(tiles):
                even[(plane,) + cell(i, j)] = src[(plane,) + cell(i, j)]

    def pair(t, carry):
        k = 2 * t + 1
        advance(odd, even, tiles)
        advance(even, odd, tiles)
        add_orders(even, odd, total, cells, table, k + 1, tiles)
        return carry

    lax.fori_loop(0, ORDER // 2 - 1, pair, 0)
    advance(odd, even, tiles)
    for i in range(SUB):
        for j in range(tiles):
            cr, ci = weighted(table, cells, ORDER, i, j)
            re, im = (0,) + cell(i, j), (1,) + cell(i, j)
            ur, ui = even[re], even[im]
            unit = pick(scale[...], cells[cell(i, j)])
            total[re] = (total[re] + (cr * ur - ci * ui)) * unit
            total[im] = (total[im] + (cr * ui + ci * ur)) * unit


def fold(block, turned, tiles):
    for j in range(tiles):
        turned[column(j), :] = block[:, column(j)].T
    return [turned[pl.ds(j, LANES, stride=tiles), :].T for j in range(tiles)]


def unfold(block, turned, tiles):
    for j in range(tiles):
        turned[pl.ds(j, LANES, stride=tiles), :] = block[:, column(j)].T
    return [turned[column(j), :].T for j in range(tiles)]


def cells_kernel(lane_ref, own, two, one, three, cells, natural, block, turned):
    here = lane_ref[0]
    tiles = cells.shape[1]
    rows = own.shape[1]
    strips = (here ^ 2, here, here ^ 3, here ^ 1)
    for piece, strip in zip((own, two, one, three), strips):
        at = pl.ds(pl.multiple_of(strip * rows, rows), rows)
        for level in range(LEVELS):
            for j in range(tiles):
                natural[level, j, at, :] = piece[level, :, column(j)]
    for level in range(LEVELS):
        for i in range(SUB):
            for j in range(tiles):
                block[pl.ds(64 * level + SUB * i, SUB), column(j)] = natural[
                    level, j, pl.ds(i, SUB, stride=SUB), :
                ].astype(jnp.float32)
    for j, tile in enumerate(fold(block, turned, tiles)):
        for level in range(LEVELS):
            cells[level, j] = tile[64 * level : 64 * level + 64].astype(jnp.int32)


def paired_cells_kernel(lane_ref, own, two, pair, *refs):
    cells_kernel(lane_ref, own, two, pair.at[0], pair.at[1], *refs)


def rows_out(level_total, bottom, natural, outs, here, rows):
    for j in range(bottom.shape[1]):
        for g in range(SUB):
            at = pl.ds(SUB * g, SUB)
            natural[0, j, at, :] = level_total[0, j, pl.ds(g, SUB, stride=SUB), :]
            natural[1, j, at, :] = bottom[0, j, pl.ds(g, SUB, stride=SUB), :]
            natural[2, j, at, :] = bottom[1, j, pl.ds(g, SUB, stride=SUB), :]
    for r, out in enumerate(outs):
        at = pl.ds(pl.multiple_of((here ^ r ^ 2) * rows, rows), rows)
        for plane in range(3):
            for j in range(bottom.shape[1]):
                out[plane, :, column(j)] = natural[plane, j, at, :]


def upper_kernel(
    lane_ref, w0, w1, w2, w3, cells, table, bottom, o0, o1, o2, o3,
    first, even, odd, block, turned, natural, codes, scale,
):
    here = lane_ref[0]
    rows = w0.shape[1]
    tiles = w0.shape[2] // LANES
    for r, piece in enumerate((w0, w1, w2, w3)):
        at = pl.ds(pl.multiple_of((here ^ r ^ 2) * rows, rows), rows)
        for plane in range(2):
            for j in range(tiles):
                natural[plane, j, at, :] = piece[plane, :, column(j)]
    for plane in range(2):
        for i in range(SUB):
            for j in range(tiles):
                block[pl.ds(64 * plane + SUB * i, SUB), column(j)] = natural[
                    plane, j, pl.ds(i, SUB, stride=SUB), :
                ]
    for j, tile in enumerate(fold(block, turned, tiles)):
        for plane in range(2):
            bottom[plane, j] = tile[64 * plane : 64 * plane + 64]
    packed(table, codes, scale)
    one_level(bottom, even, odd, first, cells.at[0], codes, scale, tiles)
    one_level(first, even, odd, bottom, cells.at[1], codes, scale, tiles)
    rows_out(first, bottom, natural, (o0, o1, o2, o3), here, rows)


def lower_kernel(
    lane_ref, wave, cells, table, o0, o1, o2, o3, first, second, even, odd, natural, codes, scale
):
    here = lane_ref[0]
    tiles = wave.shape[1]
    packed(table, codes, scale)
    one_level(wave, even, odd, first, cells.at[0], codes, scale, tiles)
    one_level(first, even, odd, second, cells.at[1], codes, scale, tiles)
    rows_out(first, second, natural, (o0, o1, o2, o3), here, o0.shape[1])


def image_kernel(lane_ref, m0, m1, m2, m3, n0, n1, n2, n3, raw, squares, turned, picture):
    top = lane_ref[1] == 0
    rows = m0.shape[1]
    tiles = m0.shape[2] // LANES
    sums = []
    for level in range(LEVELS):
        early = (n0[level] + n1[level]) + (n2[level] + n3[level])
        late = (m0[level] + m1[level]) + (m2[level] + m3[level])
        total = jnp.where(top, early, early + late)
        picture[pl.ds(rows * level, rows), :] = total
        sums.append(jnp.sum(total * total))
    lane = lax.broadcasted_iota(jnp.int32, (SUB, LANES), 1)
    squares[...] = jnp.where(lane == 0, sums[0], jnp.where(lane == 1, sums[1], 0.0))
    for level in range(LEVELS):
        raw[level] = picture[pl.ds(rows * level, rows), :]


def handed_kernel(
    lane_ref, m0, m1, m2, m3, n0, n1, n2, n3, raw, handed, image, block, turned, picture
):
    here, top = lane_ref[0], lane_ref[1] == 0
    rows = m0.shape[1]
    tiles = m0.shape[2] // LANES
    for r, (m, n) in enumerate(zip((m0, m1, m2, m3), (n0, n1, n2, n3))):
        at = (here ^ r) * (2 * rows)
        for plane in range(2):
            block[pl.ds(pl.multiple_of(at + plane * rows, rows), rows), :] = jnp.where(
                top, n[1 + plane], m[1 + plane]
            )
    for j, tile in enumerate(unfold(block, turned, tiles)):
        for f in range(NFREQ):
            for plane in range(2):
                start = (2 * f + plane) * rows
                handed[f, plane, :, column(j)] = tile[start : start + rows]
    for level in range(LEVELS):
        picture[pl.ds(rows * level, rows), :] = raw[level]
    for j, tile in enumerate(unfold(picture, turned, tiles)):
        for level in range(LEVELS):
            image[level, :, column(j)] = tile[rows * level : rows * level + rows]


def scale_kernel(cells_ref, raw, s0, s1, s2, s3, image):
    mean = ((s0[...] + s1[...]) + (s2[...] + s3[...])) / cells_ref[0].astype(jnp.float32)
    root = jnp.sqrt(mean + 1e-06)
    for level in range(LEVELS):
        image[level] = raw[level] / root[0:1, level : level + 1]


def call(kernel, outs, scratch, operands, moved=0):
    vmem = pl.BlockSpec(memory_space=pltpu.VMEM)
    smem = pl.BlockSpec(memory_space=pltpu.SMEM)
    return pl.pallas_call(
        kernel,
        out_shape=outs,
        in_specs=[smem] + [vmem] * (len(operands) - 1),
        out_specs=[vmem] * len(outs),
        scratch_shapes=scratch,
        compiler_params=pltpu.CompilerParams(vmem_limit_bytes=40 << 20),
        cost_estimate=pl.CostEstimate(flops=moved // 4, bytes_accessed=moved, transcendentals=0),
    )(*operands)


def frequency_shards(
    incoming_wave,
    speed_class_map,
    spectral_entry_index,
    filter_weights,
    scaled_pulsations,
    inverse_speed_classes,
):
    devices = lax.axis_size("strip")
    rows, columns = incoming_wave.shape[2], incoming_wave.shape[3]
    me = lax.axis_index("strip")
    plane, here = me // NFREQ, me % NFREQ
    planes = devices // NFREQ

    def place(p, lane):
        return (p % planes) * NFREQ + lane

    everyone = [(p, lane) for p in range(planes) for lane in range(NFREQ)]

    def send(value, pairs):
        return lax.ppermute(value, "strip", pairs)

    def in_plane(r):
        return [(place(p, n), place(p, n ^ r)) for p, n in everyone]

    def shifted(r):
        return [(place(p, n), place(p + n // 2, n ^ r)) for p, n in everyone]

    far = send(
        speed_class_map,
        [(place(p, lane), place(p + (1 if lane >= 2 else -1), lane)) for p, lane in everyone],
    )
    waves = [lax.dynamic_index_in_dim(incoming_wave, here ^ r, 0, keepdims=False) for r in range(NFREQ)]
    starts = [send(waves[r], shifted(r)) for r in (0, 1)]
    upper_half = here >= 2
    upper = jnp.where(upper_half, far, speed_class_map)
    lower = jnp.where(upper_half, speed_class_map, far)
    upper, spectral_entry_index, *crossing = lax.optimization_barrier(
        (upper, spectral_entry_index, waves[2], waves[3])
    )
    across_chip = send(upper, in_plane(2))
    starts += [send(v, shifted(r)) for r, v in zip((2, 3), crossing)]
    lanes = jnp.stack([here, (plane - jnp.where(upper_half, 0, 1)) % planes]).astype(jnp.int32)
    shape = jax.ShapeDtypeStruct
    field = (2, columns // LANES, SUB * SUB, LANES)
    half = pltpu.VMEM(field, jnp.float32)
    natural = pltpu.VMEM((3,) + field[1:], jnp.float32)
    turned = pltpu.VMEM((columns, LANES), jnp.float32)
    block = pltpu.VMEM((LANES, columns), jnp.float32)
    codes = pltpu.VMEM((ORDER + 1, SUB, LANES), jnp.int32)
    scale = pltpu.VMEM((SUB, LANES), jnp.float32)
    message = shape((3, rows, columns), jnp.float32)
    field_bytes = 4 * 2 * SUB * SUB * columns

    def folded_cells(kernel, *pieces):
        return call(
            kernel,
            [shape((LEVELS,) + field[1:], jnp.int32)],
            [pltpu.VMEM((LEVELS,) + field[1:], jnp.int32), block, turned],
            (lanes, *pieces),
            4 * field_bytes,
        )[0]

    section = (plane - 1) % planes
    entry = spectral_entry_index[section, here]
    weights = lax.dynamic_index_in_dim(filter_weights, entry, 0, keepdims=False)
    pulsation = scaled_pulsations[entry]
    angle = pulsation * inverse_speed_classes
    cosine, sine = jnp.cos(angle)[:, None], jnp.sin(angle)[:, None]
    sign = 1.0 - 2.0 * (jnp.arange(ORDER + 1) % 2).astype(jnp.float32)
    real = (weights[:, 0] * cosine - weights[:, 1] * sine) * sign
    imag = (weights[:, 0] * sine + weights[:, 1] * cosine) * sign
    table = jnp.stack([real, imag], axis=0).transpose(2, 0, 1)
    table = jnp.pad(table, ((0, 0), (0, 0), (0, LANES - NBIN)))
    table = jnp.broadcast_to(table[:, :, None, :], (ORDER + 1, 2, SUB, LANES))
    core_pair = send(jnp.stack([upper, across_chip]), in_plane(1))
    upper_cells = folded_cells(paired_cells_kernel, upper, across_chip, core_pair)
    lower, upper_cells = lax.optimization_barrier((lower, upper_cells))
    lower_pieces = [lower] + [send(lower, in_plane(r)) for r in (2, 1, 3)]
    bottom, *early = call(
        upper_kernel,
        [shape(field, jnp.float32)] + [message] * NFREQ,
        [half, half, half, block, turned, natural, codes, scale],
        (lanes, *starts, upper_cells, table),
        80 * field_bytes,
    )
    early, lower_pieces = lax.optimization_barrier((early, lower_pieces))
    early = [
        send(v, [(place(p, n), place(p - (n ^ r) // 2, n ^ r)) for p, n in everyone])
        for r, v in enumerate(early)
    ]
    lower_cells = folded_cells(cells_kernel, *lower_pieces)
    late = call(
        lower_kernel,
        [message] * NFREQ,
        [half, half, half, half, natural, codes, scale],
        (lanes, bottom, lower_cells, table),
        80 * field_bytes,
    )
    late, early = lax.optimization_barrier((late, early))
    late = [
        send(v, [(place(p, n), place(p + 1 - (n ^ r) // 2, n ^ r)) for p, n in everyone])
        for r, v in enumerate(late)
    ]
    raw, squares = call(
        image_kernel,
        [shape(speed_class_map.shape, jnp.float32), shape((SUB, LANES), jnp.float32)],
        [turned, block],
        (lanes, *late, *early),
        2 * field_bytes,
    )
    handed, raw = call(
        handed_kernel,
        [shape(incoming_wave.shape, jnp.float32), shape(speed_class_map.shape, jnp.float32)],
        [block, turned, block],
        (lanes, *late, *early, raw),
        8 * field_bytes,
    )

    def owner(s, strip):
        return place(s + strip // 2, strip ^ 2)

    sums = [squares] + [
        send(
            squares,
            [(owner(s, strip), owner(s, strip ^ r)) for s in range(planes) for strip in range(NFREQ)],
        )
        for r in range(1, NFREQ)
    ]
    section_cells = jnp.full((1,), rows * NFREQ * columns, jnp.int32)
    (image,) = call(
        scale_kernel, [shape(raw.shape, jnp.float32)], [], (section_cells, raw, *sums), field_bytes
    )
    return (image, handed)


def shards(*operands):
    lateral_count = lax.axis_size("strip") // SECTIONS
    rows, columns = operands[0].shape[2:]
    if lateral_count == NFREQ and rows * lateral_count == SUB * SUB and columns == SUB * LANES:
        return frequency_shards(*operands)
    return strip_shards(*operands)


def solution(mesh):
    return jax.shard_map(
        shards,
        mesh=mesh,
        in_specs=(
            P("groups", None, "strip", None),
            P("groups", "strip", None),
            P("groups", None),
            P(),
            P(),
            P(),
        ),
        out_specs=(P("groups", "strip", None), P("groups", None, "strip", None)),
        check_vma=False,
    )
```

```python
import functools

import jax
import jax.numpy as jnp
from jax import lax
from jax.experimental import pallas as pl
from jax.experimental.pallas import tpu as pltpu
from jax.sharding import PartitionSpec as P

SECTIONS = 4
LEVELS = 2
ORDER = 12
NFREQ = 4
NBIN = 16
NW = 16


def extended_2(shard, sides, width):
    for axis, dim in sides:
        devices, length = (lax.axis_size(axis), shard.shape[dim])
        up = [(i, (i + 1) % devices) for i in range(devices)]
        down = [(j, i) for i, j in up]
        last = lax.slice_in_dim(shard, length - width, length, axis=dim)
        initial = lax.slice_in_dim(shard, 0, width, axis=dim)
        before = lax.ppermute(last, axis, up)
        after = lax.ppermute(initial, axis, down)
        shard = jnp.concatenate([before, shard, after], axis=dim)
    return shard


def from_behind(shard, axis, by):
    devices = lax.axis_size(axis)
    return lax.ppermute(shard, axis, [(i, (i + by) % devices) for i in range(devices)])


def stencil_padded(padded):
    vertical = padded[:, :, :-2, :] + padded[:, :, 2:, :]
    middle = padded[:, :, 1:-1, :]
    return (
        -0.5 * middle[..., 1:-1]
        + 0.25 * (vertical[..., 1:-1] + middle[..., :-2] + middle[..., 2:])
        + 0.125 * (vertical[..., :-2] + vertical[..., 2:])
    )


def complex_times(coeff, field):
    real_part = coeff[:, 0] * field[:, 0] - coeff[:, 1] * field[:, 1]
    imag_part = coeff[:, 0] * field[:, 1] + coeff[:, 1] * field[:, 0]
    return jnp.stack([real_part, imag_part], axis=1)


def strip_shards(
    incoming_wave,
    speed_class_map,
    spectral_entry_index,
    filter_weights,
    scaled_pulsations,
    inverse_speed_classes,
):
    highest = lax.Precision.HIGHEST
    summed_along = incoming_wave.shape[2]
    summed_across = incoming_wave.shape[3]
    strip_count = lax.axis_size("strip")
    lateral_count = strip_count // SECTIONS
    position = (lax.axis_index("strip") - lateral_count // 2) % strip_count
    vertical_slab = position // lateral_count
    lateral_place = position % lateral_count
    section_rows = summed_along * lateral_count
    section_cells = section_rows * summed_across
    margin = ORDER
    extended_rows = summed_along + 2 * margin
    lateral_rows = (
        lateral_place * summed_along - margin + jnp.arange(extended_rows, dtype=jnp.int32)
    )
    inside = ((lateral_rows >= 0) & (lateral_rows < section_rows)).astype(jnp.float32)[
        None, None, :, None
    ]

    def mcclellan_step(field):
        padded = jnp.pad(field, ((0, 0), (0, 0), (1, 1), (0, 0)))
        padded = jnp.pad(padded, ((0, 0), (0, 0), (0, 0), (1, 1)))
        result = stencil_padded(padded)
        result = result * inside
        return result

    def interior(field):
        return field[:, :, margin : margin + summed_along, :]

    def image_downward(field, batch_index):
        freq_row = lax.dynamic_index_in_dim(spectral_entry_index, batch_index, 0, keepdims=False)
        freq_select = (freq_row[:, None] == jnp.arange(NW, dtype=jnp.int32)[None, :]).astype(
            jnp.float32
        )
        freq_coeffs = jnp.einsum("fw,wbck->fbck", freq_select, filter_weights, precision=highest)
        freq_omega = jnp.dot(freq_select, scaled_pulsations, precision=highest)
        wavefield = field
        raws = []
        for level in range(LEVELS):
            cells = speed_class_map[level].reshape(-1)
            bin_onehot = (cells[None, :] == jnp.arange(NBIN, dtype=jnp.int32)[:, None]).astype(
                jnp.float32
            )
            cell_slowness = jnp.dot(inverse_speed_classes, bin_onehot, precision=highest).reshape(
                summed_along, summed_across
            )
            table = jnp.einsum("fbck,bn->kfcn", freq_coeffs, bin_onehot, precision=highest).reshape(
                ORDER + 1, NFREQ, 2, summed_along, summed_across
            )
            extended = extended_2(wavefield, (("strip", 2),), ORDER) * inside
            previous = extended
            current = mcclellan_step(extended)
            accumulated = complex_times(table[0], interior(previous)) + complex_times(
                table[1], interior(current)
            )

            def recursion_step(order_index, state_tuple):
                before, present, running = state_tuple
                following = 2.0 * mcclellan_step(present) - before
                coeff = lax.dynamic_index_in_dim(table, order_index, 0, keepdims=False)
                running = running + complex_times(coeff, interior(following))
                return (present, following, running)

            previous, current, accumulated = lax.fori_loop(
                2, ORDER + 1, recursion_step, (previous, current, accumulated)
            )
            phase_angle = freq_omega[:, None, None] * cell_slowness[None]
            cosine = jnp.cos(phase_angle)
            sine_part = jnp.sin(phase_angle)
            real_part = accumulated[:, 0] * cosine - accumulated[:, 1] * sine_part
            imag_part = accumulated[:, 0] * sine_part + accumulated[:, 1] * cosine
            wavefield = jnp.stack([real_part, imag_part], axis=1)
            raws.append(jnp.sum(real_part, axis=0))
        return (wavefield, raws)

    above_floor_lines, above_unscaled_waves = image_downward(incoming_wave, vertical_slab)
    arriving = from_behind(above_floor_lines, "strip", lateral_count)
    second_bottom, second_raws = image_downward(arriving, jnp.maximum(vertical_slab - 1, 0))
    handed = jnp.where(vertical_slab == 0, above_floor_lines, second_bottom)
    first_section = (vertical_slab > 0).astype(jnp.float32)
    totals = [
        above_unscaled_waves[level] + first_section * second_raws[level] for level in range(LEVELS)
    ]
    selector = (jnp.arange(SECTIONS, dtype=jnp.int32) == vertical_slab).astype(jnp.float32)
    images = []
    for level in range(LEVELS):
        raw_image = totals[level]
        spread = lax.psum(selector * jnp.sum(raw_image * raw_image), "strip")
        mean_square = jnp.sum(spread * selector) / section_cells
        images.append(raw_image / jnp.sqrt(mean_square + 1e-06))
    return (jnp.stack(images, axis=0), handed)


LANES = 128
SUB = 8


def cell(i, j):
    return (j, pl.ds(SUB * i, SUB), slice(None))


def column(j):
    return pl.ds(LANES * j, LANES)


def rim(src, plane, tiles):
    sub = lax.broadcasted_iota(jnp.int32, (SUB, LANES), 0)
    lower, upper, rows = [], [], []
    for j in range(tiles):
        v0 = src[(plane,) + cell(0, j)]
        v7 = src[(plane,) + cell(SUB - 1, j)]
        p = v7 + jnp.where(sub == SUB - 1, 0.0, pltpu.roll(v0, SUB - 1, 0))
        lower.append(p)
        upper.append(jnp.where(sub == 0, v0, pltpu.roll(p, 1, 0)))
        rows.append(v0)
    return lower, upper, rows


def across(w):
    lane = lax.broadcasted_iota(jnp.int32, (SUB, LANES), 1)
    tiles = len(w)
    q = [w[j] + w[j + 1] for j in range(tiles - 1)]
    q.append(w[-1] + jnp.where(lane == LANES - 1, 0.0, pltpu.roll(w[0], LANES - 1, 1)))
    before = jnp.where(lane == 0, w[0], pltpu.roll(q[-1], 1, 1))
    return [q[j] + (q[j - 1] if j else before) for j in range(tiles)]


def pick(table, index):
    numbers = lax.GatherDimensionNumbers(
        offset_dims=(),
        collapsed_slice_dims=(1,),
        start_index_map=(1,),
        operand_batching_dims=(0,),
        start_indices_batching_dims=(0,),
    )
    return lax.gather(
        table,
        index[..., None],
        numbers,
        slice_sizes=(1, 1),
        mode=lax.GatherScatterMode.PROMISE_IN_BOUNDS,
    )


def weighted(table, cells, k, i, j):
    code = pick(table[k], cells[cell(i, j)])
    return code.astype(jnp.float32), (code << 16).astype(jnp.float32)


def advance(src, other, tiles, first=False):
    for plane in range(2):
        seam, above, present = rim(src, plane, tiles)
        for i in range(SUB):
            if i < SUB - 1:
                below = [src[(plane,) + cell(i + 1, j)] for j in range(tiles)]
                pairs = [present[j] + below[j] for j in range(tiles)]
            else:
                below, pairs = None, seam
            h = across([pairs[j] + above[j] for j in range(tiles)])
            above = pairs
            for j in range(tiles):
                at = (plane,) + cell(i, j)
                v = present[j]
                other[at] = v - 0.125 * h[j] if first else (v + v) - (0.25 * h[j] + other[at])
            present = below


def add_orders(lower, upper, total, cells, table, k, tiles, first=False):
    for i in range(SUB):
        for j in range(tiles):
            c0r, c0i = weighted(table, cells, k, i, j)
            c1r, c1i = weighted(table, cells, k + 1, i, j)
            re, im = (0,) + cell(i, j), (1,) + cell(i, j)
            ur, ui = upper[re], upper[im]
            vr, vi = lower[re], lower[im]
            a = (c1r * ur - c1i * ui) + (c0r * vr - c0i * vi)
            b = (c1r * ui + c1i * ur) + (c0r * vi + c0i * vr)
            if first:
                total[re], total[im] = a, b
            else:
                total[re] = total[re] + a
                total[im] = total[im] + b


def packed(table, codes, scale):
    largest = jnp.zeros((SUB, LANES), jnp.float32)
    for k in range(ORDER + 1):
        for part in range(2):
            largest = jnp.maximum(largest, jnp.abs(table[k, part]))
    largest = jnp.where(largest > 0, largest, 1.0)
    for k in range(ORDER + 1):
        low = jnp.round(table[k, 1] / largest * 32767.0)
        high = jnp.round(table[k, 0] / largest * 32767.0 - low / 65536.0)
        codes[k] = high.astype(jnp.int32) * 65536 + low.astype(jnp.int32)
    scale[...] = largest / (32767.0 * 65536.0)


def one_level(src, even, odd, total, cells, table, scale, tiles):
    advance(src, odd, tiles, first=True)
    add_orders(src, odd, total, cells, table, 0, tiles, first=True)
    for plane in range(2):
        for i in range(SUB):
            for j in range(tiles):
                even[(plane,) + cell(i, j)] = src[(plane,) + cell(i, j)]

    def pair(t, carry):
        k = 2 * t + 1
        advance(odd, even, tiles)
        advance(even, odd, tiles)
        add_orders(even, odd, total, cells, table, k + 1, tiles)
        return carry

    lax.fori_loop(0, ORDER // 2 - 1, pair, 0)
    advance(odd, even, tiles)
    for i in range(SUB):
        for j in range(tiles):
            cr, ci = weighted(table, cells, ORDER, i, j)
            re, im = (0,) + cell(i, j), (1,) + cell(i, j)
            ur, ui = even[re], even[im]
            unit = pick(scale[...], cells[cell(i, j)])
            total[re] = (total[re] + (cr * ur - ci * ui)) * unit
            total[im] = (total[im] + (cr * ui + ci * ur)) * unit


def fold(block, turned, tiles):
    for j in range(tiles):
        turned[column(j), :] = block[:, column(j)].T
    return [turned[pl.ds(j, LANES, stride=tiles), :].T for j in range(tiles)]


def unfold(block, turned, tiles):
    for j in range(tiles):
        turned[pl.ds(j, LANES, stride=tiles), :] = block[:, column(j)].T
    return [turned[column(j), :].T for j in range(tiles)]


def cells_kernel(lane_ref, own, two, one, three, cells, natural, block, turned):
    here = lane_ref[0]
    tiles = cells.shape[1]
    rows = own.shape[1]
    strips = (here ^ 2, here, here ^ 3, here ^ 1)
    for piece, strip in zip((own, two, one, three), strips):
        at = pl.ds(pl.multiple_of(strip * rows, rows), rows)
        for level in range(LEVELS):
            for j in range(tiles):
                natural[level, j, at, :] = piece[level, :, column(j)]
    for level in range(LEVELS):
        for i in range(SUB):
            for j in range(tiles):
                block[pl.ds(64 * level + SUB * i, SUB), column(j)] = natural[
                    level, j, pl.ds(i, SUB, stride=SUB), :
                ].astype(jnp.float32)
    for j, tile in enumerate(fold(block, turned, tiles)):
        for level in range(LEVELS):
            cells[level, j] = tile[64 * level : 64 * level + 64].astype(jnp.int32)


def paired_cells_kernel(lane_ref, own, two, pair, *refs):
    cells_kernel(lane_ref, own, two, pair.at[0], pair.at[1], *refs)


def rows_out(level_total, bottom, natural, outs, here, rows):
    for j in range(bottom.shape[1]):
        for g in range(SUB):
            at = pl.ds(SUB * g, SUB)
            natural[0, j, at, :] = level_total[0, j, pl.ds(g, SUB, stride=SUB), :]
            natural[1, j, at, :] = bottom[0, j, pl.ds(g, SUB, stride=SUB), :]
            natural[2, j, at, :] = bottom[1, j, pl.ds(g, SUB, stride=SUB), :]
    for r, out in enumerate(outs):
        at = pl.ds(pl.multiple_of((here ^ r ^ 2) * rows, rows), rows)
        for plane in range(3):
            for j in range(bottom.shape[1]):
                out[plane, :, column(j)] = natural[plane, j, at, :]


def upper_kernel(
    lane_ref, w0, w1, w2, w3, cells, table, bottom, o0, o1, o2, o3,
    first, even, odd, block, turned, natural, codes, scale,
):
    here = lane_ref[0]
    rows = w0.shape[1]
    tiles = w0.shape[2] // LANES
    for r, piece in enumerate((w0, w1, w2, w3)):
        at = pl.ds(pl.multiple_of((here ^ r ^ 2) * rows, rows), rows)
        for plane in range(2):
            for j in range(tiles):
                natural[plane, j, at, :] = piece[plane, :, column(j)]
    for plane in range(2):
        for i in range(SUB):
            for j in range(tiles):
                block[pl.ds(64 * plane + SUB * i, SUB), column(j)] = natural[
                    plane, j, pl.ds(i, SUB, stride=SUB), :
                ]
    for j, tile in enumerate(fold(block, turned, tiles)):
        for plane in range(2):
            bottom[plane, j] = tile[64 * plane : 64 * plane + 64]
    packed(table, codes, scale)
    one_level(bottom, even, odd, first, cells.at[0], codes, scale, tiles)
    one_level(first, even, odd, bottom, cells.at[1], codes, scale, tiles)
    rows_out(first, bottom, natural, (o0, o1, o2, o3), here, rows)


def lower_kernel(
    lane_ref, wave, cells, table, o0, o1, o2, o3, first, second, even, odd, natural, codes, scale
):
    here = lane_ref[0]
    tiles = wave.shape[1]
    packed(table, codes, scale)
    one_level(wave, even, odd, first, cells.at[0], codes, scale, tiles)
    one_level(first, even, odd, second, cells.at[1], codes, scale, tiles)
    rows_out(first, second, natural, (o0, o1, o2, o3), here, o0.shape[1])


def image_kernel(lane_ref, m0, m1, m2, m3, n0, n1, n2, n3, raw, squares, turned, picture):
    top = lane_ref[1] == 0
    rows = m0.shape[1]
    tiles = m0.shape[2] // LANES
    sums = []
    for level in range(LEVELS):
        early = (n0[level] + n1[level]) + (n2[level] + n3[level])
        late = (m0[level] + m1[level]) + (m2[level] + m3[level])
        total = jnp.where(top, early, early + late)
        picture[pl.ds(rows * level, rows), :] = total
        sums.append(jnp.sum(total * total))
    lane = lax.broadcasted_iota(jnp.int32, (SUB, LANES), 1)
    squares[...] = jnp.where(lane == 0, sums[0], jnp.where(lane == 1, sums[1], 0.0))
    for level in range(LEVELS):
        raw[level] = picture[pl.ds(rows * level, rows), :]


def handed_kernel(
    lane_ref, m0, m1, m2, m3, n0, n1, n2, n3, raw, handed, image, block, turned, picture
):
    here, top = lane_ref[0], lane_ref[1] == 0
    rows = m0.shape[1]
    tiles = m0.shape[2] // LANES
    for r, (m, n) in enumerate(zip((m0, m1, m2, m3), (n0, n1, n2, n3))):
        at = (here ^ r) * (2 * rows)
        for plane in range(2):
            block[pl.ds(pl.multiple_of(at + plane * rows, rows), rows), :] = jnp.where(
                top, n[1 + plane], m[1 + plane]
            )
    for j, tile in enumerate(unfold(block, turned, tiles)):
        for f in range(NFREQ):
            for plane in range(2):
                start = (2 * f + plane) * rows
                handed[f, plane, :, column(j)] = tile[start : start + rows]
    for level in range(LEVELS):
        picture[pl.ds(rows * level, rows), :] = raw[level]
    for j, tile in enumerate(unfold(picture, turned, tiles)):
        for level in range(LEVELS):
            image[level, :, column(j)] = tile[rows * level : rows * level + rows]


def scale_kernel(cells_ref, raw, s0, s1, s2, s3, image):
    mean = ((s0[...] + s1[...]) + (s2[...] + s3[...])) / cells_ref[0].astype(jnp.float32)
    root = jnp.sqrt(mean + 1e-06)
    for level in range(LEVELS):
        image[level] = raw[level] / root[0:1, level : level + 1]


def call(kernel, outs, scratch, operands, moved=0):
    vmem = pl.BlockSpec(memory_space=pltpu.VMEM)
    smem = pl.BlockSpec(memory_space=pltpu.SMEM)
    return pl.pallas_call(
        kernel,
        out_shape=outs,
        in_specs=[smem] + [vmem] * (len(operands) - 1),
        out_specs=[vmem] * len(outs),
        scratch_shapes=scratch,
        compiler_params=pltpu.CompilerParams(vmem_limit_bytes=40 << 20),
        cost_estimate=pl.CostEstimate(flops=moved // 4, bytes_accessed=moved, transcendentals=0),
    )(*operands)


def frequency_shards(
    incoming_wave,
    speed_class_map,
    spectral_entry_index,
    filter_weights,
    scaled_pulsations,
    inverse_speed_classes,
):
    devices = lax.axis_size("strip")
    rows, columns = incoming_wave.shape[2], incoming_wave.shape[3]
    me = lax.axis_index("strip")
    plane, here = me // NFREQ, me % NFREQ
    planes = devices // NFREQ

    def place(p, lane):
        return (p % planes) * NFREQ + lane

    everyone = [(p, lane) for p in range(planes) for lane in range(NFREQ)]

    def send(value, pairs):
        return lax.ppermute(value, "strip", pairs)

    def in_plane(r):
        return [(place(p, n), place(p, n ^ r)) for p, n in everyone]

    def shifted(r):
        return [(place(p, n), place(p + n // 2, n ^ r)) for p, n in everyone]

    far = send(
        speed_class_map,
        [(place(p, lane), place(p + (1 if lane >= 2 else -1), lane)) for p, lane in everyone],
    )
    waves = [lax.dynamic_index_in_dim(incoming_wave, here ^ r, 0, keepdims=False) for r in range(NFREQ)]
    starts = [send(waves[r], shifted(r)) for r in (0, 1)]
    upper_half = here >= 2
    upper = jnp.where(upper_half, far, speed_class_map)
    lower = jnp.where(upper_half, speed_class_map, far)
    upper, spectral_entry_index, *crossing = lax.optimization_barrier(
        (upper, spectral_entry_index, waves[2], waves[3])
    )
    across_chip = send(upper, in_plane(2))
    starts += [send(v, shifted(r)) for r, v in zip((2, 3), crossing)]
    lanes = jnp.stack([here, (plane - jnp.where(upper_half, 0, 1)) % planes]).astype(jnp.int32)
    shape = jax.ShapeDtypeStruct
    field = (2, columns // LANES, SUB * SUB, LANES)
    half = pltpu.VMEM(field, jnp.float32)
    natural = pltpu.VMEM((3,) + field[1:], jnp.float32)
    turned = pltpu.VMEM((columns, LANES), jnp.float32)
    block = pltpu.VMEM((LANES, columns), jnp.float32)
    codes = pltpu.VMEM((ORDER + 1, SUB, LANES), jnp.int32)
    scale = pltpu.VMEM((SUB, LANES), jnp.float32)
    message = shape((3, rows, columns), jnp.float32)
    field_bytes = 4 * 2 * SUB * SUB * columns

    def folded_cells(kernel, *pieces):
        return call(
            kernel,
            [shape((LEVELS,) + field[1:], jnp.int32)],
            [pltpu.VMEM((LEVELS,) + field[1:], jnp.int32), block, turned],
            (lanes, *pieces),
            4 * field_bytes,
        )[0]

    section = (plane - 1) % planes
    entry = spectral_entry_index[section, here]
    weights = lax.dynamic_index_in_dim(filter_weights, entry, 0, keepdims=False)
    pulsation = scaled_pulsations[entry]
    angle = pulsation * inverse_speed_classes
    cosine, sine = jnp.cos(angle)[:, None], jnp.sin(angle)[:, None]
    sign = 1.0 - 2.0 * (jnp.arange(ORDER + 1) % 2).astype(jnp.float32)
    real = (weights[:, 0] * cosine - weights[:, 1] * sine) * sign
    imag = (weights[:, 0] * sine + weights[:, 1] * cosine) * sign
    table = jnp.stack([real, imag], axis=0).transpose(2, 0, 1)
    table = jnp.pad(table, ((0, 0), (0, 0), (0, LANES - NBIN)))
    table = jnp.broadcast_to(table[:, :, None, :], (ORDER + 1, 2, SUB, LANES))
    core_pair = send(jnp.stack([upper, across_chip]), in_plane(1))
    upper_cells = folded_cells(paired_cells_kernel, upper, across_chip, core_pair)
    lower, upper_cells = lax.optimization_barrier((lower, upper_cells))
    lower_pieces = [lower] + [send(lower, in_plane(r)) for r in (2, 1, 3)]
    bottom, *early = call(
        upper_kernel,
        [shape(field, jnp.float32)] + [message] * NFREQ,
        [half, half, half, block, turned, natural, codes, scale],
        (lanes, *starts, upper_cells, table),
        80 * field_bytes,
    )
    early, lower_pieces = lax.optimization_barrier((early, lower_pieces))
    early = [
        send(v, [(place(p, n), place(p - (n ^ r) // 2, n ^ r)) for p, n in everyone])
        for r, v in enumerate(early)
    ]
    lower_cells = folded_cells(cells_kernel, *lower_pieces)
    late = call(
        lower_kernel,
        [message] * NFREQ,
        [half, half, half, half, natural, codes, scale],
        (lanes, bottom, lower_cells, table),
        80 * field_bytes,
    )
    late, early = lax.optimization_barrier((late, early))
    late = [
        send(v, [(place(p, n), place(p + 1 - (n ^ r) // 2, n ^ r)) for p, n in everyone])
        for r, v in enumerate(late)
    ]
    raw, squares = call(
        image_kernel,
        [shape(speed_class_map.shape, jnp.float32), shape((SUB, LANES), jnp.float32)],
        [turned, block],
        (lanes, *late, *early),
        2 * field_bytes,
    )
    handed, raw = call(
        handed_kernel,
        [shape(incoming_wave.shape, jnp.float32), shape(speed_class_map.shape, jnp.float32)],
        [block, turned, block],
        (lanes, *late, *early, raw),
        8 * field_bytes,
    )

    def owner(s, strip):
        return place(s + strip // 2, strip ^ 2)

    sums = [squares] + [
        send(
            squares,
            [(owner(s, strip), owner(s, strip ^ r)) for s in range(planes) for strip in range(NFREQ)],
        )
        for r in range(1, NFREQ)
    ]
    section_cells = jnp.full((1,), rows * NFREQ * columns, jnp.int32)
    (image,) = call(
        scale_kernel, [shape(raw.shape, jnp.float32)], [], (section_cells, raw, *sums), field_bytes
    )
    return (image, handed)


def shards(*operands):
    lateral_count = lax.axis_size("strip") // SECTIONS
    rows, columns = operands[0].shape[2:]
    if lateral_count == NFREQ and rows * lateral_count == SUB * SUB and columns == SUB * LANES:
        return frequency_shards(*operands)
    return strip_shards(*operands)


def solution(mesh):
    return jax.shard_map(
        shards,
        mesh=mesh,
        in_specs=(
            P("groups", None, "strip", None),
            P("groups", "strip", None),
            P("groups", None),
            P(),
            P(),
            P(),
        ),
        out_specs=(P("groups", "strip", None), P("groups", None, "strip", None)),
        check_vma=False,
    )
```
